128 devices in a mesh: lat: 8 (over y, core), lon: 16 (over z, x).
Axes of the slice: x: 4, y: 4, z: 4, core: 2. Of those that a mesh axis runs over, the one named last changes fastest.
Arguments:
- latents: bfloat16 [131072, 512], P(('lat', 'lon')), may hold values from -6 to 6
- d_out: bfloat16 [131072, 512], P(('lat', 'lon')), may hold values from -6 to 6
- observations: bfloat16 [4096, 8, 256], P(('lat', 'lon')), may hold values from -6 to 6
- obs_bias: bfloat16 [4096, 8], P(('lat', 'lon')), may hold values from -2 to 258
- footprint: int32 [4096, 4], P(('lat', 'lon')), may hold values from 0 to 127, all different within a row; in each aligned block of 32 rows (0 to 31, 32 to 63, ...) at most 2 rows name the same one
- obs_cell: int32 [4096, 4, 8], P(('lat', 'lon')), may hold values from 0 to 8
- w_obs: bfloat16 [256, 512], replicated, may hold values from -0.375 to 0.375
- w_kv: bfloat16 [512, 1024], replicated, may hold values from -0.25 to 0.25
- w_q: bfloat16 [512, 512], replicated, may hold values from -0.25 to 0.25
- w_o: bfloat16 [512, 512], replicated, may hold values from -0.25 to 0.25
Outputs:
- updated: bfloat16 [131072, 512], P(('lat', 'lon'))
- d_latents: bfloat16 [131072, 512], P(('lat', 'lon'))
- grad_w_obs: float32 [256, 512], replicated
- grad_w_kv: float32 [512, 1024], replicated
- grad_w_q: float32 [512, 512], replicated
- grad_w_o: float32 [512, 512], replicated
The draws below stay inside these ranges and needn't reach their ends.
Inputs may be any that keep to these rules, and one draw needn't show every extreme that they name: `footprint`: A block's 4 tiles are distinct. Among the rows of one device no tile is named more than 2 times, a bound that some block reaches. `obs_cell`: the value 8 marks an observation that falls outside that footprint tile.
All inputs are finite; a program needn't handle non-finite values.
Results may differ from the reference program's by a relative error of at most 0.0098.
Values may be sent and summed in bfloat16 or wider, within the bound.
A program may use at most 128 MiB of HBM per device.

```python
import math
import jax
import jax.numpy as jnp
import numpy as np
from jax import lax

D = 512
HEADS = 8
CH = 256
OBS = 8
BLK_DEV = 32
FOOT = 4
GROUPS = 8
Q_DEV = 1024
CAP = 2
BLOCKS = 4096
QTOT = 131072
N_LAT = 8
N_LON = 16


def draw_obs_bias(key, part):
    key = jax.random.fold_in(key, 7)
    base = jax.random.uniform(key, (BLOCKS, OBS), jnp.float32, -2.0, 2.0)
    return base.astype(jnp.bfloat16)


def set_ends(values, key, least, high):
    extent = values.shape
    index_at = [jax.random.randint(jax.random.fold_in(key, axis), (), 0, extent[axis]) for axis in range(len(extent))]
    values = values.at[tuple(index_at)].set(least)
    longest = extent.index(max(extent))
    index_at[longest] = (index_at[longest] + 1) % extent[longest]
    return values.at[tuple(index_at)].set(high)


def levels(rng, extent, cuts, smallest, top_value):
    factor_of, own = 1.0, jax.random.fold_in(rng, 6)
    for position, blocks in cuts:
        draws = jnp.exp(jax.random.uniform(jax.random.fold_in(own, position), (blocks,), jnp.float32, smallest / len(cuts), top_value / len(cuts)))
        factor_of = factor_of * jnp.repeat(draws, extent[position] // blocks).reshape([-1 if axis == position else 1 for axis in range(len(extent))])
    return factor_of


def shared_out(rng, own, number, rows, count, top, most, slope):
    ranking = jax.random.permutation(rng, count)
    crowded, ordinary = load_shares(count, rows * top, most, slope, True), load_shares(count, rows * top, most, slope, False)
    places = jnp.arange(count)

    def named(lengths, turn):
        used = int((lengths > 0).sum())
        fixed = max(1, used // 4)
        moved = fixed + (places - fixed + turn * (used - fixed)) % max(1, count - fixed)
        return jnp.zeros((count,), jnp.int32).at[ranking[jnp.where(places < fixed, places, moved)]].set(jnp.asarray(lengths, jnp.int32))

    lengths = jnp.where(number % 4 == 0, named(crowded, number // 4), named(ordinary, number - number // 4 - 1))
    mixed = jax.random.permutation(jax.random.fold_in(own, 3), count)
    giver, sink = mixed[0:count // 2 * 2:2], mixed[1:count // 2 * 2:2]
    room = jnp.minimum(lengths[giver] - 1, most - lengths[sink]) // 2
    room = jnp.where((giver == ranking[0]) | (sink == ranking[0]) | (lengths[sink] == 0), 0, jnp.maximum(room, 0))
    moved = jax.random.randint(jax.random.fold_in(own, 4), (count // 2,), 0, 1 << 20) % (room + 1)
    lengths = lengths.at[giver].add(-moved).at[sink].add(moved)
    members = jnp.searchsorted(jnp.cumsum(lengths), jnp.arange(rows * top), side="right").astype(jnp.int32)
    listing = members.reshape(top, rows).T
    listing = listing[jax.random.permutation(jax.random.fold_in(own, 1), rows)]
    turn = jax.random.randint(jax.random.fold_in(own, 2), (rows, 1), 0, top)
    return jnp.take_along_axis(listing, (jnp.arange(top)[None, :] + turn) % top, axis=1)


def load_shares(number_of, total, bound, lean, full):
    loads = [(1 << 20) // math.isqrt(rank ** lean) + 1 for rank in range(1, number_of + 1)]
    largest = bound if full else min(bound, max(-(-total // number_of), total * loads[0] // sum(loads)))
    least = 1 if total - largest >= number_of - 1 else 0
    counts, rest = [largest] + [least] * (number_of - 1), total - largest - least * (number_of - 1)
    while rest > 0:
        movable = [i for i in range(1, number_of) if counts[i] < largest] or [i for i in range(1, number_of) if counts[i] < bound]
        mass, budget = sum([loads[i] for i in movable]), rest
        for i in movable:
            more = min(bound - counts[i], max(1, budget * loads[i] // mass), rest)
            counts[i] = counts[i] + more
            rest = rest - more
    return np.array(counts)


def centred(stream_key, extent, scale, bound, split=(), kind=jnp.bfloat16):
    drawn = scale * jax.random.normal(stream_key, extent, jnp.float32)
    if split:
        drawn = drawn * levels(stream_key, extent, split, -0.22, 0.18)
    return jnp.clip(drawn, -bound, bound).astype(kind)


def setup_inputs(seed: int = 0) -> dict:
    key_list = jax.random.split(jax.random.key(seed), 11)
    latents = centred(key_list[0], (QTOT, D), 1.0, 6.0, ((0, 128),))
    d_out = centred(key_list[1], (QTOT, D), 1.0, 6.0, ((0, 128),))
    observations = centred(key_list[2], (BLOCKS, OBS, CH), 1.0, 6.0, ((0, 128),))
    obs_bias = draw_obs_bias(jax.random.fold_in(key_list[10], 71), 0)
    footprint_keys = jax.random.split(jax.random.fold_in(key_list[4], 1), BLOCKS // BLK_DEV)
    footprint_turns = jax.random.permutation(jax.random.fold_in(key_list[4], 3), BLOCKS // BLK_DEV)
    footprint = jax.vmap(lambda own, number: shared_out(jax.random.fold_in(key_list[4], 2), own, number, BLK_DEV, N_LAT * N_LON, FOOT, CAP, 2))(footprint_keys, footprint_turns).reshape((BLOCKS, FOOT))
    obs_cell = set_ends(jax.random.randint(key_list[5], (BLOCKS, FOOT, OBS), 0, GROUPS + 1), jax.random.fold_in(key_list[5], 1), 0, GROUPS).astype(jnp.int32)
    w_obs = centred(key_list[6], (CH, D), CH ** -0.5, 0.375)
    w_kv = centred(key_list[7], (D, 2 * D), D ** -0.5, 0.25)
    w_q = centred(key_list[8], (D, D), D ** -0.5, 0.25)
    w_o = centred(key_list[9], (D, D), D ** -0.5, 0.25)
    return dict(latents=latents, d_out=d_out, observations=observations, obs_bias=obs_bias, footprint=footprint, obs_cell=obs_cell, w_obs=w_obs, w_kv=w_kv, w_q=w_q, w_o=w_o)


def gelu_value(x):
    return 0.5 * x * (1.0 + jax.scipy.special.erf(x / math.sqrt(2.0)))

def gelu_slope(x):
    return 0.5 * (1.0 + jax.scipy.special.erf(x / math.sqrt(2.0))) + x * jnp.exp(-0.5 * x * x) / math.sqrt(2.0 * math.pi)

def slot_ranks(foot_local, devices):
    flat = foot_local.reshape(-1).astype(jnp.int32)
    onehot = (flat[:, None] == jnp.arange(devices, dtype=jnp.int32)[None, :]).astype(jnp.int32)
    running = jnp.cumsum(onehot, axis=0)
    rank = lax.optimization_barrier(jnp.sum(running * onehot, axis=1)) - 1
    return (flat, rank.astype(jnp.int32))

def split_heads(x):
    return x.reshape(x.shape[0], HEADS, -1).transpose(1, 0, 2)

def merge_heads(x):
    return x.transpose(1, 0, 2).reshape(x.shape[1], -1)

def slot_grads(rows_s, pre_s, enc_s, dkeyval, w_kv):
    grad_kv = jnp.dot(enc_s.T, dkeyval, preferred_element_type=jnp.float32)
    d_enc = jnp.dot(dkeyval, w_kv.T, preferred_element_type=jnp.float32)
    d_pre = (d_enc * gelu_slope(pre_s)).astype(jnp.bfloat16)
    grad_obs = jnp.dot(rows_s.T, d_pre, preferred_element_type=jnp.float32)
    return (grad_obs, grad_kv)

def attend(lat, dout, keyval, cells, bias, w_q, w_o):
    q_rows = lat.shape[0]
    width = w_q.shape[0]
    scale = 1.0 / math.sqrt(width // HEADS)
    query = jnp.dot(lat, w_q, preferred_element_type=jnp.float32).astype(jnp.bfloat16)
    back = jnp.dot(dout, w_o.T, preferred_element_type=jnp.float32).astype(jnp.bfloat16)
    group = jnp.arange(q_rows, dtype=jnp.int32) // (q_rows // GROUPS)
    visible = group[:, None] == cells[None, :]

    def per_head(inputs):
        qh, kh, vh, dh = inputs
        score = jnp.dot(qh, kh.T, preferred_element_type=jnp.float32) * scale + bias[None, :]
        top = jnp.maximum(lax.optimization_barrier(jnp.max(jnp.where(visible, score, -jnp.inf), axis=1)), 0.0)
        expd = jnp.where(visible, jnp.exp(jnp.where(visible, score, 0.0) - top[:, None]), 0.0)
        denom = jnp.exp(-top) + lax.optimization_barrier(jnp.sum(expd, axis=1))
        weights = expd / denom[:, None]
        weights_b = weights.astype(jnp.bfloat16)
        attn_h = jnp.dot(weights_b, vh, preferred_element_type=jnp.float32)
        dprob = jnp.dot(dh, vh.T, preferred_element_type=jnp.float32)
        delta = lax.optimization_barrier(jnp.sum(weights * dprob, axis=1, keepdims=True))
        dscore = (weights * (dprob - delta)).astype(jnp.bfloat16)
        dq_h = jnp.dot(dscore, kh, preferred_element_type=jnp.float32) * scale
        dk_h = jnp.dot(dscore.T, qh, preferred_element_type=jnp.float32) * scale
        dv_h = jnp.dot(weights_b.T, dh, preferred_element_type=jnp.float32)
        return (attn_h, dq_h, dk_h, dv_h)
    heads_out = lax.map(per_head, (split_heads(query), split_heads(keyval[:, :width]), split_heads(keyval[:, width:]), split_heads(back)))
    attn = merge_heads(heads_out[0]).astype(jnp.bfloat16)
    updated = (lat.astype(jnp.float32) + jnp.dot(attn, w_o, preferred_element_type=jnp.float32)).astype(jnp.bfloat16)
    grad_o = jnp.dot(attn.T, dout, preferred_element_type=jnp.float32)
    dquery = merge_heads(heads_out[1]).astype(jnp.bfloat16)
    grad_q = jnp.dot(lat.T, dquery, preferred_element_type=jnp.float32)
    d_lat = (dout.astype(jnp.float32) + jnp.dot(dquery, w_q.T, preferred_element_type=jnp.float32)).astype(jnp.bfloat16)
    dkeyval = jnp.concatenate([merge_heads(heads_out[2]), merge_heads(heads_out[3])], axis=1).astype(jnp.bfloat16)
    return (updated, d_lat, dkeyval, grad_q, grad_o)

def reference(latents, d_out, observations, obs_bias, footprint, obs_cell, w_obs, w_kv, w_q, w_o):
    devices = N_LAT * N_LON
    rows = observations.reshape(BLOCKS * OBS, CH)
    pre = jnp.dot(rows, w_obs, preferred_element_type=jnp.float32)
    enc = gelu_value(pre).astype(jnp.bfloat16)
    keyval = jnp.dot(enc, w_kv, preferred_element_type=jnp.float32).astype(jnp.bfloat16).reshape(BLOCKS, OBS, 2 * D)
    pre_b = pre.reshape(BLOCKS, OBS, D)
    enc_b = enc.reshape(BLOCKS, OBS, D)
    flat, rank = jax.vmap(lambda f: slot_ranks(f, devices))(footprint.reshape(devices, BLK_DEV * FOOT))
    sender = jnp.arange(devices, dtype=jnp.int32)[:, None]
    column = sender * CAP + rank
    pair_id = jnp.arange(devices * BLK_DEV * FOOT, dtype=jnp.int32)
    table = jnp.full((devices, devices * CAP), -1, jnp.int32).at[flat.reshape(-1), column.reshape(-1)].set(pair_id)
    cells_all = obs_cell.reshape(BLOCKS * FOOT, OBS)

    def tile_step(carry, inputs):
        grad_obs, grad_kv, grad_q, grad_o = carry
        entries, lat, dout = inputs
        live = entries >= 0
        safe = jnp.maximum(entries, 0)
        block = safe // FOOT
        keys = jnp.where(live[:, None, None], keyval[block], 0.0).astype(keyval.dtype).reshape(-1, 2 * D)
        cells = jnp.where(live[:, None], cells_all[safe], GROUPS).reshape(-1).astype(jnp.int32)
        bias = jnp.where(live[:, None], obs_bias[block].astype(jnp.float32), 0.0).reshape(-1)
        rows_s = jnp.where(live[:, None, None], observations[block], 0.0).astype(jnp.bfloat16).reshape(-1, CH)
        pre_s = jnp.where(live[:, None, None], pre_b[block], 0.0).astype(jnp.float32).reshape(-1, D)
        enc_s = jnp.where(live[:, None, None], enc_b[block], 0.0).astype(jnp.bfloat16).reshape(-1, D)
        updated, d_lat, dkeyval, part_q, part_o = attend(lat, dout, keys, cells, bias, w_q, w_o)
        part_obs, part_kv = slot_grads(rows_s, pre_s, enc_s, dkeyval, w_kv)
        return ((grad_obs + part_obs, grad_kv + part_kv, grad_q + part_q, grad_o + part_o), (updated, d_lat))
    init = (jnp.zeros((CH, D), jnp.float32), jnp.zeros((D, 2 * D), jnp.float32), jnp.zeros((D, D), jnp.float32), jnp.zeros((D, D), jnp.float32))
    carry, outs = lax.scan(tile_step, init, (table, latents.reshape(devices, Q_DEV, D), d_out.reshape(devices, Q_DEV, D)))
    grad_w_obs, grad_w_kv, grad_w_q, grad_w_o = carry
    updated = outs[0].reshape(QTOT, D)
    d_latents = outs[1].reshape(QTOT, D)
    return (updated, d_latents, grad_w_obs, grad_w_kv, grad_w_q, grad_w_o)
```

```python
import functools
import math

import jax
import jax.numpy as jnp
from jax import lax
from jax.experimental import pallas as pl
from jax.experimental.pallas import tpu as pltpu
from jax.sharding import PartitionSpec as P

HEADS = 8
GROUPS = 8
DEV = 128
OBS = 8
CAP = 2
CH = 256
D = 512
CELLS = 1024
GCELLS = CELLS // GROUPS
ROWS = DEV * CAP * OBS
WIDE = CH + 128
KB = 256
MAXB = 16
F32 = jnp.float32
BF16 = jnp.bfloat16
NEG = -1e30


def dot(a, b):
    return lax.dot_general(a, b, (((1,), (0,)), ((), ())), preferred_element_type=F32)


def dot_nt(a, b):
    return lax.dot_general(a, b, (((1,), (1,)), ((), ())), preferred_element_type=F32)


def dot_tn(a, b):
    return lax.dot_general(a, b, (((0,), (0,)), ((), ())), preferred_element_type=F32)


def iota(shape, dim):
    return lax.broadcasted_iota(jnp.int32, shape, dim)


def gelu_parts(x):
    a = jnp.abs(x)
    t = 1.0 / (1.0 + (0.3275911 / math.sqrt(2.0)) * a)
    e = jnp.exp(-0.5 * x * x)
    poly = t * (
        0.5 * 0.254829592
        + t * (-0.5 * 0.284496736 + t * (0.5 * 1.421413741 + t * (-0.5 * 1.453152027 + t * (0.5 * 1.061405429))))
    )
    tail = poly * e
    cdf = jnp.where(x < 0.0, tail, 1.0 - tail)
    return x * cdf, cdf + x * e * (1.0 / math.sqrt(2.0 * math.pi))


def pack_kernel(foot_ref, obs_ref, out_ref):
    slots = DEV * CAP
    tile = iota((slots, 128), 0)
    hit = jnp.zeros((slots, 128), F32)
    for f in range(4):
        hit = hit + jnp.where(foot_ref[f : f + 1, :] == tile // CAP, 1.0, 0.0)
    upper = jnp.where(iota((128, 128), 0) < iota((128, 128), 1), 1.0, 0.0).astype(BF16)
    rank = dot(hit.astype(BF16), upper)
    sel = hit * jnp.where(rank == (tile % CAP).astype(F32), 1.0, 0.0)
    widen = jnp.where(iota((128, 256), 1) // OBS == iota((128, 256), 0), 1.0, 0.0).astype(BF16)
    blocks = dot(sel.astype(BF16), widen)
    spread = jnp.broadcast_to(blocks[:, None, :], (slots, OBS, 256)).reshape(ROWS, 256)
    keep = iota((ROWS, 256), 0) % OBS == iota((ROWS, 256), 1) % OBS
    choose = jnp.where(keep, spread, 0.0).astype(BF16)
    out_ref[...] = dot(choose, obs_ref[...]).astype(BF16)


def tile_kernel(
    recv_ref, lat_ref, dout_ref, wobs_ref, wkv_ref, wq_ref, wo_ref,
    upd_ref, dlat_ref, grads_ref,
    q_s, back_s, rows_s, slope_s, enc_s, kv_s, bias_s, attn_s, attnt_s, dq_s, meta_sm,
):
    me = lax.axis_index(("lat", "lon"))

    take = jnp.where(iota((16, 128), 0) == iota((16, 128), 1), 1.0, 0.0).astype(BF16)
    meta = dot_nt(take, recv_ref[:, CH:])
    mine = (me + 1).astype(F32)
    cell = jnp.full((1, ROWS), float(GROUPS), F32)
    for f in range(4):
        cell = jnp.where(meta[5 + f : 6 + f, :] == mine, meta[1 + f : 2 + f, :], cell)
    cell = jnp.concatenate([cell[:, i * 128 : (i + 1) * 128] for i in range(16)], axis=0)
    inside = jnp.concatenate([jnp.where(cell == float(g), 1.0, 0.0) for g in range(GROUPS)], axis=0)
    r, c = iota((128, 128), 0), iota((128, 128), 1)
    upto = jnp.where(r <= c, 1.0, 0.0).astype(BF16)
    prefix = dot(inside.astype(BF16), upto)
    total = jnp.broadcast_to(prefix[:, 127:128], (128, 128)).astype(BF16)
    same = r // 16 == c // 16
    before = dot(jnp.where(same & (c < r), 1.0, 0.0).astype(BF16), total)
    count = dot(jnp.where(same, 1.0, 0.0).astype(BF16), total)
    nblk = jnp.floor((count + (KB - 1.0)) * (1.0 / KB))
    first = dot(jnp.where((c % 16 == 0) & (c // 16 < r // 16), 1.0, 0.0).astype(BF16), nblk.astype(BF16))
    place = jnp.where(inside > 0.5, first * float(KB) + before + prefix - 1.0, -1.0)
    pos = place[0:16, :]
    for g in range(1, GROUPS):
        pos = jnp.maximum(pos, place[g * 16 : (g + 1) * 16, :])
    for g in range(GROUPS):
        meta_sm[0, g] = jnp.max(first[g * 16 : g * 16 + 8, :]).astype(jnp.int32)
        meta_sm[1, g] = jnp.max(nblk[g * 16 : g * 16 + 8, :]).astype(jnp.int32)
    blocks = meta_sm[0, GROUPS - 1] + meta_sm[1, GROUPS - 1]

    q_s[...] = (dot(lat_ref[...], wq_ref[...]).astype(BF16).astype(F32) * 0.125).astype(BF16)
    back_s[...] = dot_nt(dout_ref[...], wo_ref[...]).astype(BF16)

    lane_pos = [jnp.broadcast_to(pos[i : i + 1, :], (16, 128)) for i in range(16)]
    row_id = iota((KB, 128), 0).astype(F32).astype(BF16)

    def encode(b, carry):
        base = (b * KB).astype(F32)
        r0 = pl.multiple_of(b * KB, KB)
        cols = []
        for i in range(16):
            rel = jnp.clip(lane_pos[i] - base, -1.0, float(KB)).astype(BF16)
            rel = jnp.concatenate([rel] * (KB // 16), axis=0)
            cols.append(jnp.where(row_id == rel, jnp.ones((), BF16), jnp.zeros((), BF16)))
        got = dot(jnp.concatenate(cols, axis=1), recv_ref[...])
        rows = got[:, :CH].astype(BF16)
        bias = jnp.where(got[:, CH + 15 : CH + 16] > 0.5, got[:, CH : CH + 1], NEG)
        bias_s[pl.ds(r0, KB), :] = jnp.broadcast_to(bias, (KB, 128))
        rows_s[pl.ds(r0, KB), :] = rows
        value, slope = gelu_parts(dot(rows, wobs_ref[...]))
        enc = value.astype(BF16)
        slope_s[pl.ds(r0, KB), :] = slope
        enc_s[pl.ds(r0, KB), :] = enc
        kv_s[pl.ds(r0, KB), :] = dot(enc, wkv_ref[...]).astype(BF16)
        return carry

    lax.fori_loop(0, blocks, encode, 0)

    lane_head = iota((GCELLS, 256), 1) // 64

    def spread_heads(x):
        return jnp.concatenate([jnp.where(lane_head == h, x, jnp.zeros((), BF16)) for h in range(4)], axis=0)

    def scores(r0, half, qq):
        keys = kv_s[pl.ds(r0, KB), half * 256 : half * 256 + 256]
        bias = bias_s[pl.ds(r0, KB), :]
        return dot_nt(keys, qq) + jnp.concatenate([bias] * 4, axis=1)

    def dprobs(r0, half, bb):
        return dot_nt(kv_s[pl.ds(r0, KB), D + half * 256 : D + half * 256 + 256], bb)

    def diagonal(x):
        return jnp.concatenate([x[h * 64 : h * 64 + 64, h * 128 : h * 128 + 128] for h in range(4)], axis=0)

    def finish(r0, half, weights, dp, delta, qq, bb):
        wb = weights.astype(BF16)
        ds = (weights * (dp - delta)).astype(BF16)
        klane, vlane = half * 256, D + half * 256
        keys = kv_s[pl.ds(r0, KB), klane : klane + 256]
        values = kv_s[pl.ds(r0, KB), vlane : vlane + 256]
        attn = diagonal(dot(values.T, wb))
        dq = diagonal(dot(keys.T, ds))
        kv_s[pl.ds(r0, KB), klane : klane + 256] = dot(ds, qq).astype(BF16)
        kv_s[pl.ds(r0, KB), vlane : vlane + 256] = dot(wb, bb).astype(BF16)
        return attn, dq

    def group(g, carry):
        start, nb = meta_sm[0, g], meta_sm[1, g]
        c0 = pl.multiple_of(g * GCELLS, GCELLS)

        def put(half, attn, dq):
            lanes = slice(half * 256, half * 256 + 256)
            at = attn.astype(BF16)
            attnt_s[g, lanes, :] = at
            attn_s[pl.ds(c0, GCELLS), lanes] = at.T
            dq_s[pl.ds(c0, GCELLS), lanes] = (dq * 0.125).astype(BF16).T

        def heads(half):
            lanes = slice(half * 256, half * 256 + 256)
            return spread_heads(q_s[pl.ds(c0, GCELLS), lanes]), spread_heads(back_s[pl.ds(c0, GCELLS), lanes])

        @pl.when(nb == 1)
        def _():
            r0 = pl.multiple_of(start * KB, KB)
            for half in range(2):
                qq, bb = heads(half)
                s = scores(r0, half, qq)
                top = jnp.maximum(jnp.max(s, axis=0, keepdims=True), 0.0)
                p = jnp.exp(s - top)
                inv = 1.0 / (jnp.exp(-top) + jnp.sum(p, axis=0, keepdims=True))
                weights = p * inv
                dp = dprobs(r0, half, bb)
                delta = jnp.sum(weights * dp, axis=0, keepdims=True)
                put(half, *finish(r0, half, weights, dp, delta, qq, bb))

        @pl.when(nb != 1)
        def _():
            for half in range(2):
                qq, bb = heads(half)

                def row(b):
                    return pl.multiple_of((start + b) * KB, KB)

                def first_pass(b, top):
                    return jnp.maximum(top, jnp.max(scores(row(b), half, qq), axis=0, keepdims=True))

                top = lax.fori_loop(0, nb, first_pass, jnp.zeros((1, 512), F32))

                def second_pass(b, sums):
                    p = jnp.exp(scores(row(b), half, qq) - top)
                    dp = dprobs(row(b), half, bb)
                    return (
                        sums[0] + jnp.sum(p, axis=0, keepdims=True),
                        sums[1] + jnp.sum(p * dp, axis=0, keepdims=True),
                    )

                sums = lax.fori_loop(0, nb, second_pass, (jnp.exp(-top), jnp.zeros((1, 512), F32)))
                inv = 1.0 / sums[0]
                delta = sums[1] * inv

                def third_pass(b, acc):
                    weights = jnp.exp(scores(row(b), half, qq) - top) * inv
                    dp = dprobs(row(b), half, bb)
                    attn, dq = finish(row(b), half, weights, dp, delta, qq, bb)
                    return acc[0] + attn, acc[1] + dq

                zero = jnp.zeros((256, GCELLS), F32)
                put(half, *lax.fori_loop(0, nb, third_pass, (zero, zero)))

        return carry

    lax.fori_loop(0, GROUPS, group, 0)

    attn, dq = attn_s[...], dq_s[...]
    upd_ref[...] = (lat_ref[...].astype(F32) + dot(attn, wo_ref[...])).astype(BF16)
    dlat_ref[...] = (dout_ref[...].astype(F32) + dot_nt(dq, wq_ref[...])).astype(BF16)
    grads_ref[1280:1792, :] = dot_tn(lat_ref[...], dq)
    attnt = jnp.concatenate([attnt_s[g] for g in range(GROUPS)], axis=1)
    grads_ref[1792:2304, :] = dot(attnt, dout_ref[...])

    grads_ref[0:1280, :] = jnp.zeros((1280, D), F32)

    def encoder_grads(b, carry):
        r0 = pl.multiple_of(b * KB, KB)
        dkv = kv_s[pl.ds(r0, KB), :]
        denc = dot_nt(dkv, wkv_ref[...])
        dpre = (denc * slope_s[pl.ds(r0, KB), :]).astype(BF16)
        grads_ref[0:256, :] += dot_tn(rows_s[pl.ds(r0, KB), :], dpre)
        part = dot_tn(enc_s[pl.ds(r0, KB), :], dkv)
        grads_ref[256:768, :] += part[:, :D]
        grads_ref[768:1280, :] += part[:, D:]
        return carry

    lax.fori_loop(0, blocks, encoder_grads, 0)


def body(latents, d_out, observations, obs_bias, footprint, obs_cell, w_obs, w_kv, w_q, w_o):
    blocks = observations.shape[0]
    rows = blocks * OBS
    foot = jnp.pad(footprint.T, ((0, 4), (0, 128 - blocks)), constant_values=-1)
    one = jnp.ones((rows, 1), BF16)
    meta = jnp.concatenate(
        [
            obs_bias.reshape(rows, 1),
            obs_cell.transpose(0, 2, 1).reshape(rows, 4).astype(BF16),
            jnp.broadcast_to(footprint[:, None, :] + 1, (blocks, OBS, 4)).reshape(rows, 4).astype(BF16),
            jnp.zeros((rows, 6), BF16),
            one,
            jnp.zeros((rows, 112), BF16),
        ],
        axis=1,
    )
    wide = jnp.concatenate([observations.reshape(rows, CH), meta], axis=1)
    vmem = pl.BlockSpec(memory_space=pltpu.VMEM)
    payload = pl.pallas_call(
        pack_kernel,
        out_shape=jax.ShapeDtypeStruct((ROWS, WIDE), BF16),
        in_specs=[vmem] * 2,
        out_specs=vmem,
        compiler_params=pltpu.CompilerParams(vmem_limit_bytes=40 << 20),
        name="pack",
    )(foot, wide)
    recv = lax.all_to_all(payload, ("lat", "lon"), split_axis=0, concat_axis=0, tiled=True)
    upd, dlat, grads = pl.pallas_call(
        tile_kernel,
        out_shape=(
            jax.ShapeDtypeStruct((CELLS, D), BF16),
            jax.ShapeDtypeStruct((CELLS, D), BF16),
            jax.ShapeDtypeStruct((2304, D), F32),
        ),
        in_specs=[vmem] * 7,
        out_specs=(vmem, vmem, vmem),
        scratch_shapes=[
            pltpu.VMEM((CELLS, D), BF16),
            pltpu.VMEM((CELLS, D), BF16),
            pltpu.VMEM((MAXB * KB, CH), BF16),
            pltpu.VMEM((MAXB * KB, D), F32),
            pltpu.VMEM((MAXB * KB, D), BF16),
            pltpu.VMEM((MAXB * KB, 2 * D), BF16),
            pltpu.VMEM((MAXB * KB, 128), F32),
            pltpu.VMEM((CELLS, D), BF16),
            pltpu.VMEM((GROUPS, D, GCELLS), BF16),
            pltpu.VMEM((CELLS, D), BF16),
            pltpu.SMEM((2, GROUPS), jnp.int32),
        ],
        compiler_params=pltpu.CompilerParams(vmem_limit_bytes=60 << 20),
        name="tile",
    )(recv, latents, d_out, w_obs, w_kv, w_q, w_o)
    grads = lax.psum(grads, ("lat", "lon"))
    gkv = jnp.concatenate([grads[256:768], grads[768:1280]], axis=1)
    return upd, dlat, grads[0:256], gkv, grads[1280:1792], grads[1792:2304]


def solution(mesh):
    spread = ("lat", "lon")
    placed = (
        P(spread, None), P(spread, None), P(spread, None, None), P(spread, None), P(spread, None),
        P(spread, None, None), P(), P(), P(), P(),
    )
    return jax.shard_map(
        body,
        mesh=mesh,
        in_specs=placed,
        out_specs=(P(spread, None), P(spread, None), P(), P(), P(), P()),
        check_vma=False,
    )
```

```python
import functools
import math

import jax
import jax.numpy as jnp
from jax import lax
from jax.experimental import pallas as pl
from jax.experimental.pallas import tpu as pltpu
from jax.sharding import PartitionSpec as P

HEADS = 8
GROUPS = 8
DEV = 128
OBS = 8
CAP = 2
CH = 256
D = 512
CELLS = 1024
GCELLS = CELLS // GROUPS
ROWS = DEV * CAP * OBS
WIDE = CH + 128
KB = 256
MAXB = 16
F32 = jnp.float32
BF16 = jnp.bfloat16
NEG = -1e30
MESH = pl.DeviceIdType.MESH


def dot(a, b):
    return lax.dot_general(a, b, (((1,), (0,)), ((), ())), preferred_element_type=F32)


def dot_nt(a, b):
    return lax.dot_general(a, b, (((1,), (1,)), ((), ())), preferred_element_type=F32)


def dot_tn(a, b):
    return lax.dot_general(a, b, (((0,), (0,)), ((), ())), preferred_element_type=F32)


def iota(shape, dim):
    return lax.broadcasted_iota(jnp.int32, shape, dim)


def gelu_parts(x):
    a = jnp.abs(x)
    t = 1.0 / (1.0 + (0.3275911 / math.sqrt(2.0)) * a)
    e = jnp.exp(-0.5 * x * x)
    poly = t * (
        0.5 * 0.254829592
        + t * (-0.5 * 0.284496736 + t * (0.5 * 1.421413741 + t * (-0.5 * 1.453152027 + t * (0.5 * 1.061405429))))
    )
    tail = poly * e
    cdf = jnp.where(x < 0.0, tail, 1.0 - tail)
    return x * cdf, cdf + x * e * (1.0 / math.sqrt(2.0 * math.pi))


def pack_kernel(foot_ref, obs_ref, out_ref):
    slots = DEV * CAP
    tile = iota((slots, 128), 0)
    hit = jnp.zeros((slots, 128), F32)
    for f in range(4):
        hit = hit + jnp.where(foot_ref[f : f + 1, :] == tile // CAP, 1.0, 0.0)
    upper = jnp.where(iota((128, 128), 0) < iota((128, 128), 1), 1.0, 0.0).astype(BF16)
    rank = dot(hit.astype(BF16), upper)
    sel = hit * jnp.where(rank == (tile % CAP).astype(F32), 1.0, 0.0)
    widen = jnp.where(iota((128, 256), 1) // OBS == iota((128, 256), 0), 1.0, 0.0).astype(BF16)
    blocks = dot(sel.astype(BF16), widen)
    spread = jnp.broadcast_to(blocks[:, None, :], (slots, OBS, 256)).reshape(ROWS, 256)
    keep = iota((ROWS, 256), 0) % OBS == iota((ROWS, 256), 1) % OBS
    choose = jnp.where(keep, spread, 0.0).astype(BF16)
    out_ref[...] = dot(choose, obs_ref[...]).astype(BF16)


def tile_kernel(
    recv_ref, lat_ref, dout_ref, wobs_ref, wkv_ref, wq_ref, wo_ref,
    upd_ref, dlat_ref, grads_ref,
    q_s, back_s, rows_s, slope_s, enc_s, kv_s, bias_s, attn_s, attnt_s, dq_s, sums_s, meta_sm,
):
    me = lax.axis_index(("lat", "lon"))

    take = jnp.where(iota((16, 128), 0) == iota((16, 128), 1), 1.0, 0.0).astype(BF16)
    meta = dot_nt(take, recv_ref[:, CH:])
    mine = (me + 1).astype(F32)
    cell = jnp.full((1, ROWS), float(GROUPS), F32)
    for f in range(4):
        cell = jnp.where(meta[5 + f : 6 + f, :] == mine, meta[1 + f : 2 + f, :], cell)
    cell = jnp.concatenate([cell[:, i * 128 : (i + 1) * 128] for i in range(16)], axis=0)
    inside = jnp.concatenate([jnp.where(cell == float(g), 1.0, 0.0) for g in range(GROUPS)], axis=0)
    r, c = iota((128, 128), 0), iota((128, 128), 1)
    upto = jnp.where(r <= c, 1.0, 0.0).astype(BF16)
    prefix = dot(inside.astype(BF16), upto)
    total = jnp.broadcast_to(prefix[:, 127:128], (128, 128)).astype(BF16)
    same = r // 16 == c // 16
    before = dot(jnp.where(same & (c < r), 1.0, 0.0).astype(BF16), total)
    count = dot(jnp.where(same, 1.0, 0.0).astype(BF16), total)
    nblk = jnp.floor((count + (KB - 1.0)) * (1.0 / KB))
    first = dot(jnp.where((c % 16 == 0) & (c // 16 < r // 16), 1.0, 0.0).astype(BF16), nblk.astype(BF16))
    place = jnp.where(inside > 0.5, first * float(KB) + before + prefix - 1.0, -1.0)
    pos = place[0:16, :]
    for g in range(1, GROUPS):
        pos = jnp.maximum(pos, place[g * 16 : (g + 1) * 16, :])
    for g in range(GROUPS):
        meta_sm[0, g] = jnp.max(first[g * 16 : g * 16 + 8, :]).astype(jnp.int32)
        meta_sm[1, g] = jnp.max(nblk[g * 16 : g * 16 + 8, :]).astype(jnp.int32)
    blocks = meta_sm[0, GROUPS - 1] + meta_sm[1, GROUPS - 1]

    q_s[...] = (dot(lat_ref[...], wq_ref[...]).astype(BF16).astype(F32) * 0.125).astype(BF16)
    back_s[...] = dot_nt(dout_ref[...], wo_ref[...]).astype(BF16)

    lane_pos = [jnp.broadcast_to(pos[i : i + 1, :], (16, 128)) for i in range(16)]
    row_id = iota((KB, 128), 0).astype(F32).astype(BF16)

    def encode(b, carry):
        base = (b * KB).astype(F32)
        r0 = pl.multiple_of(b * KB, KB)
        cols = []
        for i in range(16):
            rel = jnp.clip(lane_pos[i] - base, -1.0, float(KB)).astype(BF16)
            rel = jnp.concatenate([rel] * (KB // 16), axis=0)
            cols.append(jnp.where(row_id == rel, jnp.ones((), BF16), jnp.zeros((), BF16)))
        got = dot(jnp.concatenate(cols, axis=1), recv_ref[...])
        rows = got[:, :CH].astype(BF16)
        bias = jnp.where(got[:, CH + 15 : CH + 16] > 0.5, got[:, CH : CH + 1], NEG)
        bias_s[pl.ds(r0, KB), :] = jnp.broadcast_to(bias, (KB, 128))
        rows_s[pl.ds(r0, KB), :] = rows
        value, slope = gelu_parts(dot(rows, wobs_ref[...]))
        enc = value.astype(BF16)
        slope_s[pl.ds(r0, KB), :] = slope
        enc_s[pl.ds(r0, KB), :] = enc
        kv_s[pl.ds(r0, KB), :] = dot(enc, wkv_ref[...]).astype(BF16)
        return carry

    lax.fori_loop(0, blocks, encode, 0)

    lane_head = iota((GCELLS, 256), 1) // 64

    def spread_heads(x):
        return jnp.concatenate([jnp.where(lane_head == h, x, jnp.zeros((), BF16)) for h in range(4)], axis=0)

    def scores(r0, half, qq):
        keys = kv_s[pl.ds(r0, KB), half * 256 : half * 256 + 256]
        bias = bias_s[pl.ds(r0, KB), :]
        return dot_nt(keys, qq) + jnp.concatenate([bias] * 4, axis=1)

    def dprobs(r0, half, bb):
        return dot_nt(kv_s[pl.ds(r0, KB), D + half * 256 : D + half * 256 + 256], bb)

    def diagonal(x):
        return jnp.concatenate([x[h * 64 : h * 64 + 64, h * 128 : h * 128 + 128] for h in range(4)], axis=0)

    def finish(r0, half, weights, dp, delta, qq, bb):
        wb = weights.astype(BF16)
        ds = (weights * (dp - delta)).astype(BF16)
        klane, vlane = half * 256, D + half * 256
        keys = kv_s[pl.ds(r0, KB), klane : klane + 256]
        values = kv_s[pl.ds(r0, KB), vlane : vlane + 256]
        attn = diagonal(dot(values.T, wb))
        dq = diagonal(dot(keys.T, ds))
        kv_s[pl.ds(r0, KB), klane : klane + 256] = dot(ds, qq).astype(BF16)
        kv_s[pl.ds(r0, KB), vlane : vlane + 256] = dot(wb, bb).astype(BF16)
        return attn, dq

    def group(g, carry):
        start, nb = meta_sm[0, g], meta_sm[1, g]
        c0 = pl.multiple_of(g * GCELLS, GCELLS)

        def put(half, attn, dq):
            lanes = slice(half * 256, half * 256 + 256)
            at = attn.astype(BF16)
            attnt_s[g, lanes, :] = at
            attn_s[pl.ds(c0, GCELLS), lanes] = at.T
            dq_s[pl.ds(c0, GCELLS), lanes] = (dq * 0.125).astype(BF16).T

        def heads(half):
            lanes = slice(half * 256, half * 256 + 256)
            return spread_heads(q_s[pl.ds(c0, GCELLS), lanes]), spread_heads(back_s[pl.ds(c0, GCELLS), lanes])

        @pl.when(nb == 1)
        def _():
            r0 = pl.multiple_of(start * KB, KB)
            for half in range(2):
                qq, bb = heads(half)
                s = scores(r0, half, qq)
                top = jnp.maximum(jnp.max(s, axis=0, keepdims=True), 0.0)
                p = jnp.exp(s - top)
                inv = 1.0 / (jnp.exp(-top) + jnp.sum(p, axis=0, keepdims=True))
                weights = p * inv
                dp = dprobs(r0, half, bb)
                delta = jnp.sum(weights * dp, axis=0, keepdims=True)
                put(half, *finish(r0, half, weights, dp, delta, qq, bb))

        @pl.when(nb != 1)
        def _():
            for half in range(2):
                qq, bb = heads(half)

                def row(b):
                    return pl.multiple_of((start + b) * KB, KB)

                def first_pass(b, top):
                    return jnp.maximum(top, jnp.max(scores(row(b), half, qq), axis=0, keepdims=True))

                top = lax.fori_loop(0, nb, first_pass, jnp.zeros((1, 512), F32))

                def second_pass(b, sums):
                    p = jnp.exp(scores(row(b), half, qq) - top)
                    dp = dprobs(row(b), half, bb)
                    return (
                        sums[0] + jnp.sum(p, axis=0, keepdims=True),
                        sums[1] + jnp.sum(p * dp, axis=0, keepdims=True),
                    )

                sums = lax.fori_loop(0, nb, second_pass, (jnp.exp(-top), jnp.zeros((1, 512), F32)))
                inv = 1.0 / sums[0]
                delta = sums[1] * inv

                def third_pass(b, acc):
                    weights = jnp.exp(scores(row(b), half, qq) - top) * inv
                    dp = dprobs(row(b), half, bb)
                    attn, dq = finish(row(b), half, weights, dp, delta, qq, bb)
                    return acc[0] + attn, acc[1] + dq

                zero = jnp.zeros((256, GCELLS), F32)
                put(half, *lax.fori_loop(0, nb, third_pass, (zero, zero)))

        return carry

    lax.fori_loop(0, GROUPS, group, 0)

    attn, dq = attn_s[...], dq_s[...]
    upd_ref[...] = (lat_ref[...].astype(F32) + dot(attn, wo_ref[...])).astype(BF16)
    dlat_ref[...] = (dout_ref[...].astype(F32) + dot_nt(dq, wq_ref[...])).astype(BF16)
    grads_ref[1280:1792, :] = dot_tn(lat_ref[...], dq).astype(BF16)
    attnt = jnp.concatenate([attnt_s[g] for g in range(GROUPS)], axis=1)
    grads_ref[1792:2304, :] = dot(attnt, dout_ref[...]).astype(BF16)

    sums_s[...] = jnp.zeros((1280, D), F32)

    def encoder_grads(b, carry):
        r0 = pl.multiple_of(b * KB, KB)
        dkv = kv_s[pl.ds(r0, KB), :]
        denc = dot_nt(dkv, wkv_ref[...])
        dpre = (denc * slope_s[pl.ds(r0, KB), :]).astype(BF16)
        sums_s[0:256, :] += dot_tn(rows_s[pl.ds(r0, KB), :], dpre)
        part = dot_tn(enc_s[pl.ds(r0, KB), :], dkv)
        sums_s[256:768, :] += part[:, :D]
        sums_s[768:1280, :] += part[:, D:]
        return carry

    lax.fori_loop(0, blocks, encoder_grads, 0)
    grads_ref[0:1280, :] = sums_s[...].astype(BF16)


PARTS = 3
HALF = 1152
PROWS = 384
PIECE = 96


def peer(step_axis, k):
    lat, lon = lax.axis_index("lat"), lax.axis_index("lon")
    y, core, z, x = lat // 2, lat % 2, lon // 4, lon % 4
    if step_axis == "x":
        x = (x + k) % 4
    elif step_axis == "y":
        y = (y + k) % 4
    elif step_axis == "z":
        z = (z + k) % 4
    else:
        core = 1 - core
    return {"lat": y * 2 + core, "lon": z * 4 + x}


def place_on(step_axis):
    lat, lon = lax.axis_index("lat"), lax.axis_index("lon")
    return {"x": lon % 4, "y": lat // 2, "z": lon // 4}[step_axis]


def sum_kernel(
    g_ref, out_ref,
    core_recv, src1, recv1, src2, recv2, buf3, full, other,
    sem_core, sem1, sem2, sem3, sem4, sem5, sem6,
):
    core = lax.axis_index("lat") % 2
    order = ("x", "y", "z")
    barrier = pltpu.get_barrier_semaphore()
    pl.semaphore_signal(barrier, inc=1, device_id=peer("core", 1), device_id_type=MESH)
    for axis in order:
        for k in range(1, 4):
            pl.semaphore_signal(barrier, inc=1, device_id=peer(axis, k), device_id_type=MESH)
    pl.semaphore_wait(barrier, 10)

    def send(src, dst, sems, axis, k):
        copy = pltpu.make_async_remote_copy(
            src_ref=src, dst_ref=dst, send_sem=sems.at[0], recv_sem=sems.at[1],
            device_id=peer(axis, k), device_id_type=MESH,
        )
        copy.start()
        return copy

    mine = pl.multiple_of(core * HALF, HALF)
    theirs = pl.multiple_of((1 - core) * HALF, HALF)
    copies = []
    first = []
    for p in range(PARTS):
        first.append(
            send(g_ref.at[pl.ds(theirs + p * PROWS, PROWS), :], core_recv.at[p], sem_core.at[p], "core", 1)
        )
    second = []
    for p in range(PARTS):
        axis = order[p]
        first[p].wait_recv()
        for j in range(4):
            own = g_ref[pl.ds(mine + p * PROWS + j * PIECE, PIECE), :].astype(F32)
            src1[p, j] = (own + core_recv[p, j * PIECE : (j + 1) * PIECE, :].astype(F32)).astype(BF16)
        at = place_on(axis)
        second.append([
            send(src1.at[p, (at + k) % 4], recv1.at[p, k - 1], sem1.at[p, k - 1], axis, k) for k in range(1, 4)
        ])
    third = []
    for p in range(PARTS):
        axis, nxt = order[p], order[(p + 1) % 3]
        for copy in second[p]:
            copy.wait_recv()
        total = src1[p, place_on(axis)].astype(F32)
        for k in range(3):
            total = total + recv1[p, k].astype(F32)
        for j in range(4):
            src2[p, j] = total[:, j * 128 : (j + 1) * 128].astype(BF16)
        at = place_on(nxt)
        third.append([
            send(src2.at[p, (at + k) % 4], recv2.at[p, k - 1], sem2.at[p, k - 1], nxt, k) for k in range(1, 4)
        ])
    fourth = []
    for p in range(PARTS):
        axis, nxt = order[(p + 1) % 3], order[(p + 2) % 3]
        for copy in third[p]:
            copy.wait_recv()
        total = src2[p, place_on(axis)].astype(F32)
        for k in range(3):
            total = total + recv2[p, k].astype(F32)
        buf3[p, 0] = total.astype(BF16)
        fourth.append([send(buf3.at[p, 0], buf3.at[p, k], sem3.at[p, k - 1], nxt, k) for k in range(1, 4)])
    fifth = []
    for p in range(PARTS):
        a1, a2, a3 = order[p], order[(p + 1) % 3], order[(p + 2) % 3]
        for copy in fourth[p]:
            copy.wait_recv()
        at = place_on(a3)
        total = buf3[p, at].astype(F32)
        for s in range(1, 4):
            total = total + buf3[p, (at + 4 - s) % 4].astype(F32)
        i, j = place_on(a1), place_on(a2)
        full[p, i, j] = total.astype(BF16)
        fifth.append([send(full.at[p, i, j], full.at[p, i, j], sem4.at[p, k - 1], a2, k) for k in range(1, 4)])
    sixth = []
    for p in range(PARTS):
        a1 = order[p]
        for copy in fifth[p]:
            copy.wait_recv()
        i = place_on(a1)
        sixth.append([send(full.at[p, i], full.at[p, i], sem5.at[p, k - 1], a1, k) for k in range(1, 4)])
    last = []
    for p in range(PARTS):
        for copy in sixth[p]:
            copy.wait_recv()
        last.append(send(full.at[p], other.at[p], sem6.at[p], "core", 1))
        for i in range(4):
            for j in range(4):
                out_ref[pl.ds(mine + p * PROWS + i * PIECE, PIECE), j * 128 : (j + 1) * 128] = full[p, i, j]
    for p in range(PARTS):
        last[p].wait_recv()
        for i in range(4):
            for j in range(4):
                out_ref[pl.ds(theirs + p * PROWS + i * PIECE, PIECE), j * 128 : (j + 1) * 128] = other[p, i, j]
    for p in range(PARTS):
        for copy in [first[p], last[p]] + second[p] + third[p] + fourth[p] + fifth[p] + sixth[p]:
            copy.wait_send()


def widen_kernel(g_ref, obs_ref, kv_ref, q_ref, o_ref):
    obs_ref[...] = g_ref[0:256, :].astype(F32)
    kv_ref[:, :D] = g_ref[256:768, :].astype(F32)
    kv_ref[:, D:] = g_ref[768:1280, :].astype(F32)
    q_ref[...] = g_ref[1280:1792, :].astype(F32)
    o_ref[...] = g_ref[1792:2304, :].astype(F32)


def sum_grads(grads):
    vmem = pl.BlockSpec(memory_space=pltpu.VMEM)
    dma = pltpu.SemaphoreType.DMA
    return pl.pallas_call(
        sum_kernel,
        out_shape=jax.ShapeDtypeStruct((2 * HALF, D), BF16),
        in_specs=[vmem],
        out_specs=vmem,
        scratch_shapes=[
            pltpu.VMEM((PARTS, PROWS, D), BF16),
            pltpu.VMEM((PARTS, 4, PIECE, D), BF16),
            pltpu.VMEM((PARTS, 3, PIECE, D), BF16),
            pltpu.VMEM((PARTS, 4, PIECE, 128), BF16),
            pltpu.VMEM((PARTS, 3, PIECE, 128), BF16),
            pltpu.VMEM((PARTS, 4, PIECE, 128), BF16),
            pltpu.VMEM((PARTS, 4, 4, PIECE, 128), BF16),
            pltpu.VMEM((PARTS, 4, 4, PIECE, 128), BF16),
            dma((PARTS, 2)),
            dma((PARTS, 3, 2)),
            dma((PARTS, 3, 2)),
            dma((PARTS, 3, 2)),
            dma((PARTS, 3, 2)),
            dma((PARTS, 3, 2)),
            dma((PARTS, 2)),
        ],
        compiler_params=pltpu.CompilerParams(
            collective_id=1, has_side_effects=True, vmem_limit_bytes=40 << 20
        ),
        name="sum_grads",
    )(grads)


def body(latents, d_out, observations, obs_bias, footprint, obs_cell, w_obs, w_kv, w_q, w_o):
    blocks = observations.shape[0]
    rows = blocks * OBS
    foot = jnp.pad(footprint.T, ((0, 4), (0, 128 - blocks)), constant_values=-1)
    one = jnp.ones((rows, 1), BF16)
    meta = jnp.concatenate(
        [
            obs_bias.reshape(rows, 1),
            obs_cell.transpose(0, 2, 1).reshape(rows, 4).astype(BF16),
            jnp.broadcast_to(footprint[:, None, :] + 1, (blocks, OBS, 4)).reshape(rows, 4).astype(BF16),
            jnp.zeros((rows, 6), BF16),
            one,
            jnp.zeros((rows, 112), BF16),
        ],
        axis=1,
    )
    wide = jnp.concatenate([observations.reshape(rows, CH), meta], axis=1)
    vmem = pl.BlockSpec(memory_space=pltpu.VMEM)
    payload = pl.pallas_call(
        pack_kernel,
        out_shape=jax.ShapeDtypeStruct((ROWS, WIDE), BF16),
        in_specs=[vmem] * 2,
        out_specs=vmem,
        compiler_params=pltpu.CompilerParams(vmem_limit_bytes=40 << 20),
        name="pack",
    )(foot, wide)
    recv = lax.all_to_all(payload, ("lat", "lon"), split_axis=0, concat_axis=0, tiled=True)
    upd, dlat, grads = pl.pallas_call(
        tile_kernel,
        out_shape=(
            jax.ShapeDtypeStruct((CELLS, D), BF16),
            jax.ShapeDtypeStruct((CELLS, D), BF16),
            jax.ShapeDtypeStruct((2304, D), BF16),
        ),
        in_specs=[vmem] * 7,
        out_specs=(vmem, vmem, vmem),
        scratch_shapes=[
            pltpu.VMEM((CELLS, D), BF16),
            pltpu.VMEM((CELLS, D), BF16),
            pltpu.VMEM((MAXB * KB, CH), BF16),
            pltpu.VMEM((MAXB * KB, D), F32),
            pltpu.VMEM((MAXB * KB, D), BF16),
            pltpu.VMEM((MAXB * KB, 2 * D), BF16),
            pltpu.VMEM((MAXB * KB, 128), F32),
            pltpu.VMEM((CELLS, D), BF16),
            pltpu.VMEM((GROUPS, D, GCELLS), BF16),
            pltpu.VMEM((CELLS, D), BF16),
            pltpu.VMEM((1280, D), F32),
            pltpu.SMEM((2, GROUPS), jnp.int32),
        ],
        compiler_params=pltpu.CompilerParams(vmem_limit_bytes=60 << 20),
        name="tile",
    )(recv, latents, d_out, w_obs, w_kv, w_q, w_o)
    gobs, gkv, gq, go = pl.pallas_call(
        widen_kernel,
        out_shape=[jax.ShapeDtypeStruct(x.shape, F32) for x in (w_obs, w_kv, w_q, w_o)],
        in_specs=[vmem],
        out_specs=[vmem] * 4,
        compiler_params=pltpu.CompilerParams(vmem_limit_bytes=40 << 20),
        name="widen",
    )(sum_grads(grads))
    return upd, dlat, gobs, gkv, gq, go


def solution(mesh):
    spread = ("lat", "lon")
    placed = (
        P(spread, None), P(spread, None), P(spread, None, None), P(spread, None), P(spread, None),
        P(spread, None, None), P(), P(), P(), P(),
    )
    return jax.shard_map(
        body,
        mesh=mesh,
        in_specs=placed,
        out_specs=(P(spread, None), P(spread, None), P(), P(), P(), P()),
        check_vma=False,
    )
```

```python
import functools
import math

import jax
import jax.numpy as jnp
from jax import lax
from jax.experimental import pallas as pl
from jax.experimental.pallas import tpu as pltpu
from jax.sharding import PartitionSpec as P

HEADS = 8
GROUPS = 8
DEV = 128
OBS = 8
CAP = 2
CH = 256
D = 512
CELLS = 1024
GCELLS = CELLS // GROUPS
ROWS = DEV * CAP * OBS
KB = 256
MAXB = 15
LEAD = 8
F32 = jnp.float32
BF16 = jnp.bfloat16
NEG = -1e30
VMEM_LIMIT = 59 << 20
MESH = pl.DeviceIdType.MESH


def dot(a, b):
    return lax.dot_general(a, b, (((1,), (0,)), ((), ())), preferred_element_type=F32)


def dot_nt(a, b):
    return lax.dot_general(a, b, (((1,), (1,)), ((), ())), preferred_element_type=F32)


def dot_tn(a, b):
    return lax.dot_general(a, b, (((0,), (0,)), ((), ())), preferred_element_type=F32)


def iota(shape, dim):
    return lax.broadcasted_iota(jnp.int32, shape, dim)


def gelu_parts(x):
    a = jnp.abs(x)
    t = 1.0 / (1.0 + (0.3275911 / math.sqrt(2.0)) * a)
    e = jnp.exp(-0.5 * x * x)
    poly = t * (
        0.5 * 0.254829592
        + t * (-0.5 * 0.284496736 + t * (0.5 * 1.421413741 + t * (-0.5 * 1.453152027 + t * (0.5 * 1.061405429))))
    )
    tail = poly * e
    cdf = jnp.where(x < 0.0, tail, 1.0 - tail)
    return x * cdf, cdf + x * e * (1.0 / math.sqrt(2.0 * math.pi))


def hot(mask):
    return jnp.where(mask, 1.0, 0.0).astype(BF16)


def exchange_kernel(
    foot_ref, obs_ref, bias_ref, cell_ref, lat_ref, dout_ref, wq_ref, wo_ref,
    recv_ref, rmeta_ref, q_ref, back_ref,
    foot_v, obs_v, bias_v, cell_v, lat_v, dout_v, wq_v, wo_v, q_v, back_v,
    stage, mstage, osend, omsend, foot_s, marks_s, sem_in, sem_out, sem_core, sem_chip,
):
    lat, lon = lax.axis_index("lat"), lax.axis_index("lon")
    core = lax.rem(lat, 2)
    y, z, x = lat // 2, lon // 4, lax.rem(lon, 4)
    loads = []
    for i, (src, dst) in enumerate((
        (foot_ref, foot_v), (obs_ref, obs_v), (bias_ref, bias_v), (cell_ref, cell_v),
        (lat_ref, lat_v), (wq_ref, wq_v), (dout_ref, dout_v), (wo_ref, wo_v),
    )):
        loads.append(pltpu.make_async_copy(src, dst, sem_in.at[i]))
        loads[-1].start()

    ys = [lax.rem(y + d, 4) for d in range(4)]
    lons = [lax.rem(z + d // 4, 4) * 4 + lax.rem(x + d % 4, 4) for d in range(16)]
    chips = []
    for k in range(1, 64):
        cy, cl = ys[k // 16], lons[k % 16]
        chips.append((cy * 16 + cl, {"lat": cy * 2 + core, "lon": cl}))
    sibling = {"lat": y * 2 + 1 - core, "lon": lon}
    my_chip = y * 16 + lon
    barrier = pltpu.get_barrier_semaphore()
    pl.semaphore_signal(barrier, inc=1, device_id=sibling, device_id_type=MESH)
    for chip, where in chips:
        pl.semaphore_signal(barrier, inc=1, device_id=where, device_id_type=MESH)

    foot_s[...] = jnp.full((16, 128), -1.0, F32)
    marks_s[...] = jnp.zeros((128, 1280), F32)
    for load in loads[:4]:
        load.wait()
    foot_s[0:4, 0:32] = foot_v[...].astype(F32)
    for rank in range(CAP):
        lane, at = rank * OBS, rank * 640
        marks_s[lane : lane + OBS, at : at + 32] = bias_v[...].astype(F32)
        for f in range(4):
            lane, at = (CAP + rank) * OBS, rank * 640 + (1 + f) * 128
            marks_s[lane : lane + OBS, at : at + 32] = cell_v[f].astype(F32) - float(GROUPS)
    foot = foot_s[...]
    marks = marks_s[...].astype(BF16)
    r, c = iota((128, 128), 0), iota((128, 128), 1)
    upper = hot(r < c)
    widen = hot(iota((128, 256), 1) // OBS == iota((128, 256), 0))
    keep = iota((1024, 256), 0) % OBS == iota((1024, 256), 1) % OBS

    def slots_of(to_core):
        tile = (r // 32) * 32 + to_core * 16 + (r // CAP) % 16
        hit = jnp.zeros((128, 128), F32)
        for f in range(4):
            hit = hit + jnp.where(foot[f : f + 1, :] == tile.astype(F32), 1.0, 0.0)
        sel = hit * jnp.where(dot(hit.astype(BF16), upper) == (r % CAP).astype(F32), 1.0, 0.0)
        blocks = dot(sel.astype(BF16), widen)
        spread = jnp.broadcast_to(blocks[:, None, :], (128, OBS, 256)).reshape(1024, 256)
        rows = dot(jnp.where(keep, spread, 0.0).astype(BF16), obs_v[...]).astype(BF16)
        tile = iota((64, 128), 0)
        tile = ((tile // 16) * 32 + to_core * 16 + tile % 16).astype(F32)
        hits = [jnp.where(foot[f : f + 1, :] == tile, 1.0, 0.0) for f in range(4)]
        any_hit = hits[0] + hits[1] + hits[2] + hits[3]
        order = dot(any_hit.astype(BF16), upper)
        left = []
        for rank in range(CAP):
            chosen = any_hit * jnp.where(order == float(rank), 1.0, 0.0)
            left += [chosen] + [chosen * hits[f] for f in range(4)]
        meta = dot_nt(jnp.concatenate(left, axis=1).astype(BF16), marks)
        return rows.reshape(64, 16, CH), meta.reshape(64, 1, 128)

    osend[...], omsend[...] = slots_of(1 - core)
    pl.semaphore_wait(barrier, 64)

    def copy(src, dst, sems, where):
        return pltpu.make_async_remote_copy(
            src_ref=src, dst_ref=dst, send_sem=sems.at[0], recv_sem=sems.at[1], device_id=where, device_id_type=MESH,
        )

    swap = [copy(osend, stage.at[core], sem_core.at[0], sibling), copy(omsend, mstage.at[core], sem_core.at[1], sibling)]
    for part in swap:
        part.start()
    stage[core], mstage[core] = slots_of(core)
    for part in swap:
        part.wait_recv()
    for chip, where in chips:
        copy(stage.at[:, chip], recv_ref.at[:, my_chip], sem_chip.at[0], where).start()
        copy(mstage.at[:, chip], rmeta_ref.at[:, my_chip], sem_chip.at[1], where).start()
    stores = [
        pltpu.make_async_copy(stage.at[:, my_chip], recv_ref.at[:, my_chip], sem_out.at[0]),
        pltpu.make_async_copy(mstage.at[:, my_chip], rmeta_ref.at[:, my_chip], sem_out.at[1]),
    ]
    for store in stores:
        store.start()

    loads[4].wait()
    loads[5].wait()
    q_v[...] = (dot(lat_v[...], wq_v[...]).astype(BF16).astype(F32) * 0.125).astype(BF16)
    stores.append(pltpu.make_async_copy(q_v, q_ref, sem_out.at[2]))
    stores[-1].start()
    loads[6].wait()
    loads[7].wait()
    back_v[...] = dot_nt(dout_v[...], wo_v[...]).astype(BF16)
    stores.append(pltpu.make_async_copy(back_v, back_ref, sem_out.at[3]))
    stores[-1].start()

    whole = copy(stage.at[:, 0:63], recv_ref.at[:, 0:63], sem_chip.at[0], sibling)
    marks = copy(mstage.at[:, 0:63], rmeta_ref.at[:, 0:63], sem_chip.at[1], sibling)
    whole.wait_recv()
    marks.wait_recv()
    whole.wait_send()
    marks.wait_send()
    for part in swap:
        part.wait_send()
    for store in stores:
        store.wait()


def tile_kernel(
    recv_ref, rmeta_ref, q_ref, back_ref, lat_ref, dout_ref, wobs_ref, wkv_ref, wq_ref, wo_ref,
    upd_ref, dlat_ref, main_ref, part_ref, rows_ref, slope_ref, dkv_ref,
    rows_s, slope_s, enct_s, kv_s, bias_s, attn_s, attnt_s, dq_s, sums_s, main_v, part_v, upd_v, dlat_v, meta_sm,
    recv_v, rmeta_v, q_s, back_s, lat_v, dout_v, wobs_v, wkv_v, wq_v, wo_v, sem_in, sem_blk, sem_out,
):
    loads = []
    for i, (src, dst) in enumerate((
        (rmeta_ref, rmeta_v), (recv_ref, recv_v), (wobs_ref, wobs_v), (wkv_ref, wkv_v), (q_ref, q_s), (back_ref, back_s),
        (lat_ref, lat_v), (dout_ref, dout_v), (wq_ref, wq_v), (wo_ref, wo_v),
    )):
        loads.append(pltpu.make_async_copy(src, dst, sem_in.at[i]))
        loads[-1].start()

    def block_out(b, i):
        src, dst = ((rows_s, rows_ref), (slope_s, slope_ref), (kv_s, dkv_ref))[i]
        at = pl.ds(pl.multiple_of(b * KB, KB), KB)
        return pltpu.make_async_copy(src.at[at, :], dst.at[at, :], sem_blk.at[i, b])

    loads[0].wait()
    r, c = iota((128, 128), 0), iota((128, 128), 1)
    marks = rmeta_v[...].astype(BF16)
    own_lane = r % 8 == c // 16
    chunk = jnp.where(iota((16, 128), 0) == iota((16, 128), 1) // 8, 1.0, 0.0).astype(BF16)

    def laned(first_lane):
        lanes = dot(marks, jnp.where(r == c % 16 + first_lane, 1.0, 0.0).astype(BF16))
        return dot(chunk, jnp.where(own_lane, lanes, 0.0).astype(BF16))

    bias_row = laned(0)
    cell = laned(16) + float(GROUPS)
    bias_row = jnp.concatenate([bias_row[i : i + 1, :] for i in range(16)], axis=1)
    kind = iota((16, ROWS), 0)
    extra = jnp.where(kind == 0, bias_row, jnp.where(kind == 1, 1.0, 0.0)).astype(BF16)
    inside = jnp.concatenate([jnp.where(cell == float(g), 1.0, 0.0) for g in range(GROUPS)], axis=0)
    upto = jnp.where(r <= c, 1.0, 0.0).astype(BF16)
    prefix = dot(inside.astype(BF16), upto)
    total = jnp.broadcast_to(prefix[:, 127:128], (128, 128)).astype(BF16)
    same = r // 16 == c // 16
    before = dot(jnp.where(same & (c < r), 1.0, 0.0).astype(BF16), total)
    count = dot(jnp.where(same, 1.0, 0.0).astype(BF16), total)
    nblk = jnp.floor((count + (KB - 1.0)) * (1.0 / KB))
    first = dot(jnp.where((c % 16 == 0) & (c // 16 < r // 16), 1.0, 0.0).astype(BF16), nblk.astype(BF16))
    place = jnp.where(inside > 0.5, first * float(KB) + before + prefix - 1.0, -1.0)
    pos = place[0:16, :]
    for g in range(1, GROUPS):
        pos = jnp.maximum(pos, place[g * 16 : (g + 1) * 16, :])
    for g in range(GROUPS):
        meta_sm[0, g] = jnp.max(first[g * 16 : g * 16 + 8, :]).astype(jnp.int32)
        meta_sm[1, g] = jnp.max(nblk[g * 16 : g * 16 + 8, :]).astype(jnp.int32)
    blocks = meta_sm[0, GROUPS - 1] + meta_sm[1, GROUPS - 1]

    lane_pos = [jnp.broadcast_to(pos[i : i + 1, :], (16, 128)) for i in range(16)]
    row_id = iota((KB, 128), 0).astype(F32).astype(BF16)

    def encode(b, carry):
        base = (b * KB).astype(F32)
        r0 = pl.multiple_of(b * KB, KB)
        cols = []
        for i in range(16):
            rel = jnp.clip(lane_pos[i] - base, -1.0, float(KB)).astype(BF16)
            rel = jnp.concatenate([rel] * (KB // 16), axis=0)
            cols.append(jnp.where(row_id == rel, jnp.ones((), BF16), jnp.zeros((), BF16)))
        choose = jnp.concatenate(cols, axis=1)
        rows = dot(choose, recv_v[...]).astype(BF16)
        side = dot_nt(choose, extra)
        bias = jnp.where(side[:, 1:2] > 0.5, side[:, 0:1], NEG)
        bias_s[pl.ds(r0, KB), :] = jnp.broadcast_to(bias, (KB, 128))
        rows_s[pl.ds(r0, KB), :] = rows
        value, slope = gelu_parts(dot(rows, wobs_v[...]))
        enc = value.astype(BF16)
        slope_s[pl.ds(r0, KB), :] = slope.astype(BF16)
        enct_s[:, pl.ds(r0, KB)] = enc.T
        kv_s[pl.ds(r0, KB), :] = dot(enc, wkv_v[...]).astype(BF16)

        @pl.when(b < LEAD)
        def _():
            for i in range(2):
                block_out(b, i).start()

        return carry

    for load in loads[1:4]:
        load.wait()
    lax.fori_loop(0, jnp.maximum(blocks, LEAD), encode, 0)
    for load in loads[4:6]:
        load.wait()

    lane_head = iota((GCELLS, 256), 1) // 64

    def spread_heads(x):
        return jnp.concatenate([jnp.where(lane_head == h, x, jnp.zeros((), BF16)) for h in range(4)], axis=0)

    def scores(r0, half, qq):
        keys = kv_s[pl.ds(r0, KB), half * 256 : half * 256 + 256]
        bias = bias_s[pl.ds(r0, KB), :]
        return dot_nt(keys, qq) + jnp.concatenate([bias] * 4, axis=1)

    def dprobs(r0, half, bb):
        return dot_nt(kv_s[pl.ds(r0, KB), D + half * 256 : D + half * 256 + 256], bb)

    def diagonal(x):
        return jnp.concatenate([x[h * 64 : h * 64 + 64, h * 128 : h * 128 + 128] for h in range(4)], axis=0)

    def finish(r0, half, weights, dp, delta, qq, bb):
        wb = weights.astype(BF16)
        ds = (weights * (dp - delta)).astype(BF16)
        klane, vlane = half * 256, D + half * 256
        keys = kv_s[pl.ds(r0, KB), klane : klane + 256]
        values = kv_s[pl.ds(r0, KB), vlane : vlane + 256]
        attn = diagonal(dot(values.T, wb))
        dq = diagonal(dot(keys.T, ds))
        kv_s[pl.ds(r0, KB), klane : klane + 256] = dot(ds, qq).astype(BF16)
        kv_s[pl.ds(r0, KB), vlane : vlane + 256] = dot(wb, bb).astype(BF16)
        return attn, dq

    def group(g, carry):
        start, nb = meta_sm[0, g], meta_sm[1, g]
        c0 = pl.multiple_of(g * GCELLS, GCELLS)

        def put(half, attn, dq):
            lanes = slice(half * 256, half * 256 + 256)
            at = attn.astype(BF16)
            attnt_s[g, lanes, :] = at
            attn_s[pl.ds(c0, GCELLS), lanes] = at.T
            dq_s[pl.ds(c0, GCELLS), lanes] = (dq * 0.125).astype(BF16).T

        def heads(half):
            lanes = slice(half * 256, half * 256 + 256)
            return spread_heads(q_s[pl.ds(c0, GCELLS), lanes]), spread_heads(back_s[pl.ds(c0, GCELLS), lanes])

        @pl.when(nb == 1)
        def _():
            r0 = pl.multiple_of(start * KB, KB)
            for half in range(2):
                qq, bb = heads(half)
                s = scores(r0, half, qq)
                top = jnp.maximum(jnp.max(s, axis=0, keepdims=True), 0.0)
                p = jnp.exp(s - top)
                inv = 1.0 / (jnp.exp(-top) + jnp.sum(p, axis=0, keepdims=True))
                weights = p * inv
                dp = dprobs(r0, half, bb)
                delta = jnp.sum(weights * dp, axis=0, keepdims=True)
                put(half, *finish(r0, half, weights, dp, delta, qq, bb))

        @pl.when(nb != 1)
        def _():
            for half in range(2):
                qq, bb = heads(half)

                def row(b):
                    return pl.multiple_of((start + b) * KB, KB)

                def first_pass(b, top):
                    return jnp.maximum(top, jnp.max(scores(row(b), half, qq), axis=0, keepdims=True))

                top = lax.fori_loop(0, nb, first_pass, jnp.zeros((1, 512), F32))

                def second_pass(b, sums):
                    p = jnp.exp(scores(row(b), half, qq) - top)
                    dp = dprobs(row(b), half, bb)
                    return (
                        sums[0] + jnp.sum(p, axis=0, keepdims=True),
                        sums[1] + jnp.sum(p * dp, axis=0, keepdims=True),
                    )

                sums = lax.fori_loop(0, nb, second_pass, (jnp.exp(-top), jnp.zeros((1, 512), F32)))
                inv = 1.0 / sums[0]
                delta = sums[1] * inv

                def third_pass(b, acc):
                    weights = jnp.exp(scores(row(b), half, qq) - top) * inv
                    dp = dprobs(row(b), half, bb)
                    attn, dq = finish(row(b), half, weights, dp, delta, qq, bb)
                    return acc[0] + attn, acc[1] + dq

                zero = jnp.zeros((256, GCELLS), F32)
                put(half, *lax.fori_loop(0, nb, third_pass, (zero, zero)))

        def send_block(b, carry):
            block_out(b, 2).start()
            return carry

        lax.fori_loop(jnp.minimum(start, LEAD), jnp.minimum(start + nb, LEAD), send_block, 0)
        return carry

    lax.fori_loop(0, GROUPS, group, 0)

    def send_empty(b, carry):
        block_out(b, 2).start()
        return carry

    lax.fori_loop(jnp.minimum(blocks, LEAD), LEAD, send_empty, 0)

    for load in loads[6:]:
        load.wait()
    attn, dq = attn_s[...], dq_s[...]
    outs = []

    def put_out(src, dst):
        outs.append(pltpu.make_async_copy(src, dst, sem_out.at[len(outs)]))
        outs[-1].start()

    main_v[0, 0:512, :] = dot_tn(lat_v[...], dq).astype(BF16)
    attnt = jnp.concatenate([attnt_s[g] for g in range(GROUPS)], axis=1)
    main_v[1, 0:512, :] = dot(attnt, dout_v[...]).astype(BF16)

    @pl.when(blocks <= LEAD)
    def _():
        for i in range(4):
            tile = dot(enct_s[:, 0:ROWS], kv_s[0:ROWS, i * 256 : (i + 1) * 256])
            main_v[i // 2, 512:1024, i % 2 * 256 : i % 2 * 256 + 256] = tile.astype(BF16)
        part_v[...] = jnp.zeros((CH, D), BF16)

    @pl.when(blocks > LEAD)
    def _():
        for i in range(4):
            sums_s[0:512, i * 256 : (i + 1) * 256] = dot(enct_s[:, 0:ROWS], kv_s[0:ROWS, i * 256 : (i + 1) * 256])
        sums_s[512:768, 0:512] = jnp.zeros((CH, D), F32)

        def encoder_grads(b, carry):
            r0 = pl.multiple_of(b * KB, KB)
            dkv = kv_s[pl.ds(r0, KB), :]
            dpre = (dot_nt(dkv, wkv_v[...]) * slope_s[pl.ds(r0, KB), :].astype(F32)).astype(BF16)
            sums_s[0:512, :] += dot(enct_s[:, pl.ds(r0, KB)], dkv)
            sums_s[512:768, 0:512] += dot_tn(rows_s[pl.ds(r0, KB), :], dpre)
            return carry

        lax.fori_loop(LEAD, blocks, encoder_grads, 0)
        for h in range(2):
            main_v[h, 512:1024, :] = sums_s[0:512, h * 512 : (h + 1) * 512].astype(BF16)
        part_v[...] = sums_s[512:768, 0:512].astype(BF16)

    put_out(main_v, main_ref)
    put_out(part_v, part_ref)
    upd_v[...] = (lat_v[...].astype(F32) + dot(attn, wo_v[...])).astype(BF16)
    put_out(upd_v, upd_ref)
    dlat_v[...] = (dout_v[...].astype(F32) + dot_nt(dq, wq_v[...])).astype(BF16)
    put_out(dlat_v, dlat_ref)

    for i in range(3):
        for b in range(LEAD):
            block_out(b, i).wait()
    for out in outs:
        out.wait()


ORDER = ("x", "y", "z")
JOBS = (("main", 0, 384, 0), ("main", 384, 320, 1), ("main", 704, 320, 2), ("obs", 0, 64, 1), ("obs", 64, 64, 2))


def peer(step_axis, k):
    lat, lon = lax.axis_index("lat"), lax.axis_index("lon")
    y, core, z, x = lat // 2, lat % 2, lon // 4, lon % 4
    if step_axis == "x":
        x = (x + k) % 4
    elif step_axis == "y":
        y = (y + k) % 4
    elif step_axis == "z":
        z = (z + k) % 4
    else:
        core = 1 - core
    return {"lat": y * 2 + core, "lon": z * 4 + x}


def place_on(step_axis):
    lat, lon = lax.axis_index("lat"), lax.axis_index("lon")
    return {"x": lon % 4, "y": lat // 2, "z": lon // 4}[step_axis]


class Job:
    def __init__(self, source, mine, half, start, rows, turn, bufs, sems):
        self.source, self.mine, self.start, self.rows, self.piece = source, mine, start, rows, rows // 4
        self.axes = [ORDER[(turn + i) % 3] for i in range(3)]
        self.core_recv, self.src1, self.recv1, self.src2, self.recv2, self.buf3, self.full, self.other = bufs
        self.sems, self.half, self.phase, self.sent = sems, half, -1, []

    def describe(self, src, dst, axis, k):
        return pltpu.make_async_remote_copy(
            src_ref=src, dst_ref=dst, send_sem=self.sems.at[self.phase, 0], recv_sem=self.sems.at[self.phase, 1],
            device_id=peer(axis, k), device_id_type=MESH,
        )

    def swap(self):
        self.phase += 1
        at = self.source.at[1 - self.half, pl.ds(self.start, self.rows), :]
        copy = self.describe(at, self.core_recv, "core", 1)
        copy.start()
        self.sent.append(copy)

    def around(self, axis, src_of, dst_of, whole):
        self.phase += 1
        for k in range(1, 4):
            self.describe(src_of(k), dst_of(k), axis, k).start()
        self.sent.append(self.describe(whole, whole, axis, 1))

    def arrived(self):
        self.sent[-1].wait_recv()

    def scatter1(self):
        self.arrived()
        own = self.mine[self.half, self.start : self.start + self.rows, :].astype(F32)
        total = (own + self.core_recv[...].astype(F32)).astype(BF16)
        for j in range(4):
            self.src1[j] = total[j * self.piece : (j + 1) * self.piece, :]
        at = place_on(self.axes[0])
        self.around(
            self.axes[0], lambda k: self.src1.at[lax.rem(at + k, 4)], lambda k: self.recv1.at[k - 1], self.recv1
        )

    def scatter2(self):
        self.arrived()
        total = self.src1[place_on(self.axes[0])].astype(F32)
        for k in range(3):
            total = total + self.recv1[k].astype(F32)
        for j in range(4):
            self.src2[j] = total[:, j * 128 : (j + 1) * 128].astype(BF16)
        at = place_on(self.axes[1])
        self.around(
            self.axes[1], lambda k: self.src2.at[lax.rem(at + k, 4)], lambda k: self.recv2.at[k - 1], self.recv2
        )

    def exchange3(self):
        self.arrived()
        total = self.src2[place_on(self.axes[1])].astype(F32)
        for k in range(3):
            total = total + self.recv2[k].astype(F32)
        self.buf3[0] = total.astype(BF16)
        self.around(self.axes[2], lambda k: self.buf3.at[0], lambda k: self.buf3.at[k], self.buf3.at[1:4])

    def gather2(self):
        self.arrived()
        at = place_on(self.axes[2])
        total = self.buf3[at].astype(F32)
        for s in range(1, 4):
            total = total + self.buf3[lax.rem(at + 4 - s, 4)].astype(F32)
        i, j = place_on(self.axes[0]), place_on(self.axes[1])
        self.full[i, j] = total.astype(BF16)
        mine = self.full.at[i, j]
        self.around(self.axes[1], lambda k: mine, lambda k: mine, self.recv2)

    def gather1(self):
        self.arrived()
        mine = self.full.at[place_on(self.axes[0])]
        self.around(self.axes[0], lambda k: mine, lambda k: mine, self.recv1)

    def share(self, out_ref):
        self.arrived()
        self.phase += 1
        copy = self.describe(self.full, self.other, "core", 1)
        copy.start()
        self.sent.append(copy)
        self.write(out_ref, self.full, self.half)

    def write(self, out_ref, block, half):
        for i in range(4):
            for j in range(4):
                out_ref[half, self.start + i * self.piece : self.start + (i + 1) * self.piece, j * 128 : (j + 1) * 128] = block[i, j]

    def end(self, out_ref):
        self.arrived()
        self.write(out_ref, self.other, 1 - self.half)

    def settle(self):
        for copy in self.sent:
            copy.wait_send()


def sum_kernel(
    main_ref, part_ref, rows_ref, slope_ref, dkv_ref, wkv_ref,
    omain_ref, oobs_ref,
    main_v, part_v, rows_v, slope_v, dkv_v, wkv_v, gobs_v, dpre_s, omain_v, oobs_v, sem_in, sem_out, *scratch,
):
    half = lax.rem(lax.axis_index("lat"), 2)
    loads = []
    for i, (src, dst) in enumerate((
        (main_ref, main_v), (dkv_ref, dkv_v), (wkv_ref, wkv_v),
        (slope_ref, slope_v), (rows_ref, rows_v), (part_ref, part_v),
    )):
        loads.append(pltpu.make_async_copy(src, dst, sem_in.at[i]))
        loads[-1].start()
    barrier = pltpu.get_barrier_semaphore()
    pl.semaphore_signal(barrier, inc=1, device_id=peer("core", 1), device_id_type=MESH)
    for axis in ORDER:
        for k in range(1, 4):
            pl.semaphore_signal(barrier, inc=1, device_id=peer(axis, k), device_id_type=MESH)
    sources = {"main": (main_ref, main_v), "obs": (gobs_v, gobs_v)}
    outs = {"main": omain_v, "obs": oobs_v}
    jobs = {"main": [], "obs": []}
    for i, (name, start, rows, turn) in enumerate(JOBS):
        bufs = scratch[9 * i : 9 * i + 8]
        jobs[name].append(Job(*sources[name], half, start, rows, turn, bufs, scratch[9 * i + 8]))

    def step(name, what):
        for job in jobs[name]:
            if what in ("share", "end"):
                getattr(job, what)(outs[name])
            else:
                getattr(job, what)()

    def through_encoder(i):
        at = slice(i * 512, (i + 1) * 512)
        denc = dot_nt(dkv_v[at, :], wkv_v[...])
        dpre_s[at, :] = (denc * slope_v[at, :].astype(F32)).astype(BF16)

    pl.semaphore_wait(barrier, 10)
    step("main", "swap")
    for load in loads:
        load.wait()
    through_encoder(0)
    step("main", "scatter1")
    through_encoder(1)
    through_encoder(2)
    step("main", "scatter2")
    through_encoder(3)
    total = dot_tn(rows_v[...], dpre_s[...]) + part_v[...].astype(F32)
    gobs_v[0] = total[0:128].astype(BF16)
    gobs_v[1] = total[128:256].astype(BF16)
    step("obs", "swap")
    step("main", "exchange3")
    step("obs", "scatter1")
    step("main", "gather2")
    step("obs", "scatter2")
    step("main", "gather1")
    step("obs", "exchange3")
    step("obs", "gather2")
    step("main", "share")
    step("obs", "gather1")
    step("main", "end")
    store = pltpu.make_async_copy(omain_v, omain_ref, sem_out.at[0])
    store.start()
    step("obs", "share")
    step("obs", "end")
    last = pltpu.make_async_copy(oobs_v, oobs_ref, sem_out.at[1])
    last.start()
    for name in jobs:
        for job in jobs[name]:
            job.settle()
    store.wait()
    last.wait()


def widen_kernel(main_ref, gobs_ref, obs_ref, kv_ref, q_ref, o_ref):
    obs_ref[...] = gobs_ref[0].astype(F32)
    q_ref[...] = main_ref[0, 0].astype(F32)
    o_ref[...] = main_ref[1, 0].astype(F32)
    for h in range(2):
        kv_ref[:, h * D : (h + 1) * D] = main_ref[h, 1].astype(F32)


def sum_grads(main, part, rows, slope, dkv, w_kv):
    far = pl.BlockSpec(memory_space=pltpu.HBM)
    dma = pltpu.SemaphoreType.DMA
    scratch = []
    for _, _, n, _ in JOBS:
        piece = n // 4
        scratch += [
            pltpu.VMEM((n, D), BF16),
            pltpu.VMEM((4, piece, D), BF16),
            pltpu.VMEM((3, piece, D), BF16),
            pltpu.VMEM((4, piece, 128), BF16),
            pltpu.VMEM((3, piece, 128), BF16),
            pltpu.VMEM((4, piece, 128), BF16),
            pltpu.VMEM((4, 4, piece, 128), BF16),
            pltpu.VMEM((4, 4, piece, 128), BF16),
            dma((7, 2)),
        ]
    return pl.pallas_call(
        sum_kernel,
        out_shape=[jax.ShapeDtypeStruct((2, 2 * D, D), BF16), jax.ShapeDtypeStruct((2, 128, D), BF16)],
        in_specs=[far] * 6,
        out_specs=[far] * 2,
        scratch_shapes=[
            pltpu.VMEM((2, 2 * D, D), BF16),
            pltpu.VMEM((CH, D), BF16),
            pltpu.VMEM((ROWS, CH), BF16),
            pltpu.VMEM((ROWS, D), BF16),
            pltpu.VMEM((ROWS, 2 * D), BF16),
            pltpu.VMEM((D, 2 * D), BF16),
            pltpu.VMEM((2, 128, D), BF16),
            pltpu.VMEM((ROWS, D), BF16),
            pltpu.VMEM((2, 2 * D, D), BF16),
            pltpu.VMEM((2, 128, D), BF16),
            dma((6,)),
            dma((2,)),
        ] + scratch,
        compiler_params=pltpu.CompilerParams(
            collective_id=1, has_side_effects=True, vmem_limit_bytes=VMEM_LIMIT
        ),
        name="sum_grads",
    )(main, part, rows, slope, dkv, w_kv)


def body(latents, d_out, observations, obs_bias, footprint, obs_cell, w_obs, w_kv, w_q, w_o):
    vmem = pl.BlockSpec(memory_space=pltpu.VMEM)
    dma = pltpu.SemaphoreType.DMA
    far = pl.BlockSpec(memory_space=pltpu.HBM)
    recv, rmeta, q, back = pl.pallas_call(
        exchange_kernel,
        out_shape=(
            jax.ShapeDtypeStruct((2, 64, 16, CH), BF16),
            jax.ShapeDtypeStruct((2, 64, 1, 128), F32),
            jax.ShapeDtypeStruct((CELLS, D), BF16),
            jax.ShapeDtypeStruct((CELLS, D), BF16),
        ),
        in_specs=[far] * 8,
        out_specs=[far] * 4,
        scratch_shapes=[
            pltpu.VMEM((4, 32), jnp.int32),
            pltpu.VMEM((32 * OBS, CH), BF16),
            pltpu.VMEM((OBS, 32), BF16),
            pltpu.VMEM((4, OBS, 32), jnp.int32),
            pltpu.VMEM((CELLS, D), BF16),
            pltpu.VMEM((CELLS, D), BF16),
            pltpu.VMEM((D, D), BF16),
            pltpu.VMEM((D, D), BF16),
            pltpu.VMEM((CELLS, D), BF16),
            pltpu.VMEM((CELLS, D), BF16),
            pltpu.VMEM((2, 64, 16, CH), BF16),
            pltpu.VMEM((2, 64, 1, 128), F32),
            pltpu.VMEM((64, 16, CH), BF16),
            pltpu.VMEM((64, 1, 128), F32),
            pltpu.VMEM((16, 128), F32),
            pltpu.VMEM((128, 1280), F32),
            dma((8,)),
            dma((4,)),
            dma((2, 2)),
            dma((2, 2)),
        ],
        compiler_params=pltpu.CompilerParams(
            collective_id=0, has_side_effects=True, vmem_limit_bytes=VMEM_LIMIT
        ),
        name="exchange",
    )(
        footprint.T, observations.reshape(-1, CH), obs_bias.T, obs_cell.transpose(1, 2, 0),
        latents, d_out, w_q, w_o,
    )
    upd, dlat, main, part, rows, slope, dkv = pl.pallas_call(
        tile_kernel,
        out_shape=(
            jax.ShapeDtypeStruct((CELLS, D), BF16),
            jax.ShapeDtypeStruct((CELLS, D), BF16),
            jax.ShapeDtypeStruct((2, 2 * D, D), BF16),
            jax.ShapeDtypeStruct((CH, D), BF16),
            jax.ShapeDtypeStruct((ROWS, CH), BF16),
            jax.ShapeDtypeStruct((ROWS, D), BF16),
            jax.ShapeDtypeStruct((ROWS, 2 * D), BF16),
        ),
        in_specs=[far] * 10,
        out_specs=[far] * 7,
        scratch_shapes=[
            pltpu.VMEM((MAXB * KB, CH), BF16),
            pltpu.VMEM((MAXB * KB, D), BF16),
            pltpu.VMEM((D, MAXB * KB), BF16),
            pltpu.VMEM((MAXB * KB, 2 * D), BF16),
            pltpu.VMEM((MAXB * KB, 128), F32),
            pltpu.VMEM((CELLS, D), BF16),
            pltpu.VMEM((GROUPS, D, GCELLS), BF16),
            pltpu.VMEM((CELLS, D), BF16),
            pltpu.VMEM((768, 2 * D), F32),
            pltpu.VMEM((2, 2 * D, D), BF16),
            pltpu.VMEM((CH, D), BF16),
            pltpu.VMEM((CELLS, D), BF16),
            pltpu.VMEM((CELLS, D), BF16),
            pltpu.SMEM((2, GROUPS), jnp.int32),
            pltpu.VMEM((ROWS, CH), BF16),
            pltpu.VMEM((DEV, 128), F32),
            pltpu.VMEM((CELLS, D), BF16),
            pltpu.VMEM((CELLS, D), BF16),
            pltpu.VMEM((CELLS, D), BF16),
            pltpu.VMEM((CELLS, D), BF16),
            pltpu.VMEM((CH, D), BF16),
            pltpu.VMEM((D, 2 * D), BF16),
            pltpu.VMEM((D, D), BF16),
            pltpu.VMEM((D, D), BF16),
            dma((10,)),
            dma((3, LEAD)),
            dma((4,)),
        ],
        compiler_params=pltpu.CompilerParams(vmem_limit_bytes=VMEM_LIMIT),
        name="tile",
    )(recv.reshape(ROWS, CH), rmeta.reshape(DEV, 128), q, back, latents, d_out, w_obs, w_kv, w_q, w_o)
    gmain, gobs = sum_grads(main, part, rows, slope, dkv, w_kv)
    gobs, gkv, gq, go = pl.pallas_call(
        widen_kernel,
        grid=(4,),
        out_shape=[jax.ShapeDtypeStruct(x.shape, F32) for x in (w_obs, w_kv, w_q, w_o)],
        in_specs=[
            pl.BlockSpec((2, 2, 128, D), lambda i: (0, 0, i, 0)),
            pl.BlockSpec((1, 64, D), lambda i: (i // 2, i % 2, 0)),
        ],
        out_specs=[
            pl.BlockSpec((64, D), lambda i: (i, 0)),
            pl.BlockSpec((128, 2 * D), lambda i: (i, 0)),
            pl.BlockSpec((128, D), lambda i: (i, 0)),
            pl.BlockSpec((128, D), lambda i: (i, 0)),
        ],
        compiler_params=pltpu.CompilerParams(vmem_limit_bytes=VMEM_LIMIT),
        name="widen",
    )(gmain.reshape(2, 2, D, D), gobs)
    return upd, dlat, gobs, gkv, gq, go


def solution(mesh):
    spread = ("lat", "lon")
    placed = (
        P(spread, None), P(spread, None), P(spread, None, None), P(spread, None), P(spread, None),
        P(spread, None, None), P(), P(), P(), P(),
    )
    return jax.shard_map(
        body,
        mesh=mesh,
        in_specs=placed,
        out_specs=(P(spread, None), P(spread, None), P(), P(), P(), P()),
        check_vma=False,
    )
```

```python
import functools
import math

import jax
import jax.numpy as jnp
from jax import lax
from jax.experimental import pallas as pl
from jax.experimental.pallas import tpu as pltpu
from jax.sharding import PartitionSpec as P

HEADS = 8
GROUPS = 8
DEV = 128
OBS = 8
CAP = 2
CH = 256
D = 512
CELLS = 1024
GCELLS = CELLS // GROUPS
ROWS = DEV * CAP * OBS
KB = 128
MAXB = 24
LEAD = 18
SPAN = 768
F32 = jnp.float32
BF16 = jnp.bfloat16
NEG = -1e30
VMEM_LIMIT = 59 << 20
MESH = pl.DeviceIdType.MESH


def dot(a, b):
    return lax.dot_general(a, b, (((1,), (0,)), ((), ())), preferred_element_type=F32)


def dot_nt(a, b):
    return lax.dot_general(a, b, (((1,), (1,)), ((), ())), preferred_element_type=F32)


def dot_tn(a, b):
    return lax.dot_general(a, b, (((0,), (0,)), ((), ())), preferred_element_type=F32)


def iota(shape, dim):
    return lax.broadcasted_iota(jnp.int32, shape, dim)


def gelu_parts(x):
    a = jnp.abs(x)
    t = 1.0 / (1.0 + (0.3275911 / math.sqrt(2.0)) * a)
    e = jnp.exp(-0.5 * x * x)
    poly = t * (
        0.5 * 0.254829592
        + t * (-0.5 * 0.284496736 + t * (0.5 * 1.421413741 + t * (-0.5 * 1.453152027 + t * (0.5 * 1.061405429))))
    )
    tail = poly * e
    cdf = jnp.where(x < 0.0, tail, 1.0 - tail)
    return x * cdf, cdf + x * e * (1.0 / math.sqrt(2.0 * math.pi))


def hot(mask):
    return jnp.where(mask, 1.0, 0.0).astype(BF16)


def exchange_kernel(
    foot_ref, obs_ref, bias_ref, cell_ref, lat_ref, dout_ref, wq_ref, wo_ref,
    recv_ref, rmeta_ref, q_ref, back_ref,
    foot_v, obs_v, bias_v, cell_v, lat_v, dout_v, wq_v, wo_v, q_v, back_v,
    stage, mstage, osend, omsend, foot_s, marks_s, sem_in, sem_out, sem_core, sem_chip,
):
    lat, lon = lax.axis_index("lat"), lax.axis_index("lon")
    core = lax.rem(lat, 2)
    y, z, x = lat // 2, lon // 4, lax.rem(lon, 4)
    loads = []
    for i, (src, dst) in enumerate((
        (foot_ref, foot_v), (obs_ref, obs_v), (bias_ref, bias_v), (cell_ref, cell_v),
        (lat_ref, lat_v), (wq_ref, wq_v), (dout_ref, dout_v), (wo_ref, wo_v),
    )):
        loads.append(pltpu.make_async_copy(src, dst, sem_in.at[i]))
        loads[-1].start()

    ys = [lax.rem(y + d, 4) for d in range(4)]
    lons = [lax.rem(z + d // 4, 4) * 4 + lax.rem(x + d % 4, 4) for d in range(16)]
    chips = []
    for k in range(1, 64):
        cy, cl = ys[k // 16], lons[k % 16]
        chips.append((cy * 16 + cl, {"lat": cy * 2 + core, "lon": cl}))
    sibling = {"lat": y * 2 + 1 - core, "lon": lon}
    my_chip = y * 16 + lon
    barrier = pltpu.get_barrier_semaphore()
    pl.semaphore_signal(barrier, inc=1, device_id=sibling, device_id_type=MESH)
    for chip, where in chips:
        pl.semaphore_signal(barrier, inc=1, device_id=where, device_id_type=MESH)

    foot_s[...] = jnp.full((16, 128), -1.0, F32)
    marks_s[...] = jnp.zeros((128, 1280), F32)
    for load in loads[:4]:
        load.wait()
    foot_s[0:4, 0:32] = foot_v[...].astype(F32)
    for rank in range(CAP):
        lane, at = rank * OBS, rank * 640
        marks_s[lane : lane + OBS, at : at + 32] = bias_v[...].astype(F32)
        for f in range(4):
            lane, at = (CAP + rank) * OBS, rank * 640 + (1 + f) * 128
            marks_s[lane : lane + OBS, at : at + 32] = cell_v[f].astype(F32) - float(GROUPS)
    foot = foot_s[...]
    marks = marks_s[...].astype(BF16)
    r, c = iota((128, 128), 0), iota((128, 128), 1)
    upper = hot(r < c)
    widen = hot(iota((128, 256), 1) // OBS == iota((128, 256), 0))
    keep = iota((1024, 256), 0) % OBS == iota((1024, 256), 1) % OBS

    def slots_of(to_core):
        tile = (r // 32) * 32 + to_core * 16 + (r // CAP) % 16
        hit = jnp.zeros((128, 128), F32)
        for f in range(4):
            hit = hit + jnp.where(foot[f : f + 1, :] == tile.astype(F32), 1.0, 0.0)
        sel = hit * jnp.where(dot(hit.astype(BF16), upper) == (r % CAP).astype(F32), 1.0, 0.0)
        blocks = dot(sel.astype(BF16), widen)
        spread = jnp.broadcast_to(blocks[:, None, :], (128, OBS, 256)).reshape(1024, 256)
        rows = dot(jnp.where(keep, spread, 0.0).astype(BF16), obs_v[...]).astype(BF16)
        tile = iota((64, 128), 0)
        tile = ((tile // 16) * 32 + to_core * 16 + tile % 16).astype(F32)
        hits = [jnp.where(foot[f : f + 1, :] == tile, 1.0, 0.0) for f in range(4)]
        any_hit = hits[0] + hits[1] + hits[2] + hits[3]
        order = dot(any_hit.astype(BF16), upper)
        left = []
        for rank in range(CAP):
            chosen = any_hit * jnp.where(order == float(rank), 1.0, 0.0)
            left += [chosen] + [chosen * hits[f] for f in range(4)]
        meta = dot_nt(jnp.concatenate(left, axis=1).astype(BF16), marks)
        return rows.reshape(64, 16, CH), meta.reshape(64, 1, 128)

    osend[...], omsend[...] = slots_of(1 - core)
    pl.semaphore_wait(barrier, 64)

    def copy(src, dst, sems, where):
        return pltpu.make_async_remote_copy(
            src_ref=src, dst_ref=dst, send_sem=sems.at[0], recv_sem=sems.at[1], device_id=where, device_id_type=MESH,
        )

    swap = [copy(osend, stage.at[core], sem_core.at[0], sibling), copy(omsend, mstage.at[core], sem_core.at[1], sibling)]
    for part in swap:
        part.start()
    stage[core], mstage[core] = slots_of(core)
    for part in swap:
        part.wait_recv()
    for chip, where in chips:
        copy(stage.at[:, chip], recv_ref.at[:, my_chip], sem_chip.at[0], where).start()
        copy(mstage.at[:, chip], rmeta_ref.at[:, my_chip], sem_chip.at[1], where).start()
    stores = [
        pltpu.make_async_copy(stage.at[:, my_chip], recv_ref.at[:, my_chip], sem_out.at[0]),
        pltpu.make_async_copy(mstage.at[:, my_chip], rmeta_ref.at[:, my_chip], sem_out.at[1]),
    ]
    for store in stores:
        store.start()

    loads[4].wait()
    loads[5].wait()
    q_v[...] = (dot(lat_v[...], wq_v[...]).astype(BF16).astype(F32) * 0.125).astype(BF16)
    stores.append(pltpu.make_async_copy(q_v, q_ref, sem_out.at[2]))
    stores[-1].start()
    loads[6].wait()
    loads[7].wait()
    back_v[...] = dot_nt(dout_v[...], wo_v[...]).astype(BF16)
    stores.append(pltpu.make_async_copy(back_v, back_ref, sem_out.at[3]))
    stores[-1].start()

    whole = copy(stage.at[:, 0:63], recv_ref.at[:, 0:63], sem_chip.at[0], sibling)
    marks = copy(mstage.at[:, 0:63], rmeta_ref.at[:, 0:63], sem_chip.at[1], sibling)
    whole.wait_recv()
    marks.wait_recv()
    whole.wait_send()
    marks.wait_send()
    for part in swap:
        part.wait_send()
    for store in stores:
        store.wait()


def tile_kernel(
    recv_ref, rmeta_ref, q_ref, back_ref, lat_ref, dout_ref, wobs_ref, wkv_ref, wq_ref, wo_ref,
    upd_ref, dlat_ref, main_ref,
    rowst_s, slope_s, enct_s, kv_s, bias_s, attn_s, dq_s, dpre_s, sums_s, main_v, upd_v, dlat_v, meta_sm,
    recv_v, rmeta_v, q_s, back_s, lat_v, dout_v, wobs_v, wkv_v, wq_v, wo_v, sem_in, sem_out,
):
    loads = []
    for i, (src, dst) in enumerate((
        (rmeta_ref, rmeta_v), (recv_ref, recv_v), (wobs_ref, wobs_v), (wkv_ref, wkv_v), (q_ref, q_s), (back_ref, back_s),
        (lat_ref, lat_v), (dout_ref, dout_v), (wq_ref, wq_v), (wo_ref, wo_v),
    )):
        loads.append(pltpu.make_async_copy(src, dst, sem_in.at[i]))
        loads[-1].start()

    loads[0].wait()
    r, c = iota((128, 128), 0), iota((128, 128), 1)
    marks = rmeta_v[...].astype(BF16)
    own_lane = r % 8 == c // 16
    chunk = jnp.where(iota((16, 128), 0) == iota((16, 128), 1) // 8, 1.0, 0.0).astype(BF16)

    def laned(first_lane):
        lanes = dot(marks, jnp.where(r == c % 16 + first_lane, 1.0, 0.0).astype(BF16))
        return dot(chunk, jnp.where(own_lane, lanes, 0.0).astype(BF16))

    bias_row = laned(0)
    cell = laned(16) + float(GROUPS)
    inside = jnp.concatenate([jnp.where(cell == float(g), 1.0, 0.0) for g in range(GROUPS)], axis=0)
    upto = jnp.where(r <= c, 1.0, 0.0).astype(BF16)
    prefix = dot(inside.astype(BF16), upto)
    total = jnp.broadcast_to(prefix[:, 127:128], (128, 128)).astype(BF16)
    same = r // 16 == c // 16
    before = dot(jnp.where(same & (c < r), 1.0, 0.0).astype(BF16), total)
    count = dot(jnp.where(same, 1.0, 0.0).astype(BF16), total)
    nblk = jnp.floor((count + (KB - 1.0)) * (1.0 / KB))
    first = dot(jnp.where((c % 16 == 0) & (c // 16 < r // 16), 1.0, 0.0).astype(BF16), nblk.astype(BF16))
    place = jnp.where(inside > 0.5, first * float(KB) + before + prefix - 1.0, -1.0)
    pos = place[0:16, :]
    for g in range(1, GROUPS):
        pos = jnp.maximum(pos, place[g * 16 : (g + 1) * 16, :])
    for g in range(GROUPS):
        meta_sm[0, g] = jnp.max(first[g * 16 : g * 16 + 8, :]).astype(jnp.int32)
        meta_sm[1, g] = jnp.max(nblk[g * 16 : g * 16 + 8, :]).astype(jnp.int32)
        meta_sm[2, g] = jnp.max(count[g * 16 : g * 16 + 8, :]).astype(jnp.int32)
    blocks = meta_sm[0, GROUPS - 1] + meta_sm[1, GROUPS - 1]

    lane_pos = [jnp.broadcast_to(pos[i : i + 1, :], (16, 128)) for i in range(16)]
    lane_bias = [jnp.broadcast_to(bias_row[i : i + 1, :], (16, 128)).astype(BF16) for i in range(16)]
    row_id = iota((256, 128), 0).astype(F32).astype(BF16)

    def gather(base, rows):
        cols = []
        bias = jnp.zeros((rows, 128), BF16)
        for i in range(16):
            rel = jnp.clip(lane_pos[i] - base, -1.0, float(rows)).astype(BF16)
            found = row_id[0:rows] == jnp.concatenate([rel] * (rows // 16), axis=0)
            cols.append(jnp.where(found, jnp.ones((), BF16), jnp.zeros((), BF16)))
            bias = jnp.where(found, jnp.concatenate([lane_bias[i]] * (rows // 16), axis=0), bias)
        bias = jnp.sum(bias.astype(F32), axis=1, keepdims=True)
        return jnp.concatenate(cols, axis=1), jnp.broadcast_to(bias, (rows, 128))

    def picked(at, picks):
        bias_s[at, :] = jnp.concatenate([pick[1] for pick in picks], axis=0)
        rows = dot(jnp.concatenate([pick[0] for pick in picks], axis=0), recv_v[...]).astype(BF16)
        rowst_s[:, at] = rows.T
        return dot(rows, wobs_v[...])

    def encoded(at, pre):
        value, slope = gelu_parts(pre)
        enc = value.astype(BF16)
        slope_s[at, :] = slope
        enct_s[:, at] = enc.T
        kv_s[at, :] = dot(enc, wkv_v[...]).astype(BF16)

    for load in loads[1:4]:
        load.wait()
    last = None
    for i in range(LEAD * KB // SPAN):
        at = slice(i * SPAN, (i + 1) * SPAN)
        pre = picked(at, [gather(float(i * SPAN + j), 256) for j in range(0, SPAN, 256)])
        if last is not None:
            encoded(*last)
        last = (at, pre)
    encoded(*last)

    def encode(b, carry):
        at = pl.ds(pl.multiple_of(b * KB, KB), KB)
        encoded(at, picked(at, [gather((b * KB).astype(F32), KB)]))
        return carry

    lax.fori_loop(LEAD, blocks, encode, 0)
    for load in loads[4:6]:
        load.wait()

    lane_head = iota((GCELLS, 256), 1) // 64

    def spread_heads(x):
        return jnp.concatenate([jnp.where(lane_head == h, x, jnp.zeros((), BF16)) for h in range(4)], axis=0)

    def scores(r0, rows, valid, half, qq):
        keys = kv_s[pl.ds(r0, rows), half * 256 : half * 256 + 256]
        bias = jnp.where(iota((rows, 128), 0) < valid, bias_s[pl.ds(r0, rows), :], NEG)
        return dot_nt(keys, qq) + jnp.concatenate([bias] * 4, axis=1)

    def dprobs(r0, rows, half, bb):
        return dot_nt(kv_s[pl.ds(r0, rows), D + half * 256 : D + half * 256 + 256], bb)

    def diagonal(x):
        out = x[0:GCELLS]
        for h in range(1, 4):
            out = jnp.where(lane_head == h, x[h * GCELLS : (h + 1) * GCELLS], out)
        return out

    def products(r0, rows, half, wb, ds, qq, bb):
        keys = kv_s[pl.ds(r0, rows), half * 256 : half * 256 + 256]
        values = kv_s[pl.ds(r0, rows), D + half * 256 : D + half * 256 + 256]
        attn = diagonal(dot(wb.T, values))
        dq = diagonal(dot(ds.T, keys))
        return attn, dq, dot(ds, qq).astype(BF16), dot(wb, bb).astype(BF16)

    def put_keys(r0, rows, half, dk, dv):
        kv_s[pl.ds(r0, rows), half * 256 : half * 256 + 256] = dk
        kv_s[pl.ds(r0, rows), D + half * 256 : D + half * 256 + 256] = dv

    def heads(c0, half):
        lanes = slice(half * 256, half * 256 + 256)
        return spread_heads(q_s[pl.ds(c0, GCELLS), lanes]), spread_heads(back_s[pl.ds(c0, GCELLS), lanes])

    def put(c0, half, attn, dq):
        lanes = slice(half * 256, half * 256 + 256)
        attn_s[pl.ds(c0, GCELLS), lanes] = attn.astype(BF16)
        dq_s[pl.ds(c0, GCELLS), lanes] = (dq * 0.125).astype(BF16)

    def at_once(groups, rows):
        jobs = []
        for g in groups:
            r0, c0 = pl.multiple_of(meta_sm[0, g] * KB, KB), pl.multiple_of(g * GCELLS, GCELLS)
            for half in range(2):
                jobs.append((r0, c0, half, meta_sm[2, g]) + heads(c0, half))
        raw = [scores(r0, rows, valid, half, qq) for r0, _, half, valid, qq, _ in jobs]
        dps = [dprobs(r0, rows, half, bb) for r0, _, half, _, _, bb in jobs]
        done = []
        for (r0, _, half, _, qq, bb), s, dp in zip(jobs, raw, dps):
            top = jnp.maximum(jnp.max(s, axis=0, keepdims=True), 0.0)
            p = jnp.exp(s - top)
            inv = 1.0 / (jnp.exp(-top) + jnp.sum(p, axis=0, keepdims=True))
            weights = p * inv
            delta = jnp.sum(weights * dp, axis=0, keepdims=True)
            wb, ds = weights.astype(BF16), (weights * (dp - delta)).astype(BF16)
            done.append(products(r0, rows, half, wb, ds, qq, bb))
        for (r0, c0, half, _, _, _), (attn, dq, dk, dv) in zip(jobs, done):
            put_keys(r0, rows, half, dk, dv)
            put(c0, half, attn, dq)

    def by_chunks(g):
        start, nb, count = meta_sm[0, g], meta_sm[1, g], meta_sm[2, g]
        c0 = pl.multiple_of(g * GCELLS, GCELLS)
        for half in range(2):
            qq, bb = heads(c0, half)

            def row(b):
                return pl.multiple_of((start + b) * KB, KB)

            def score(b):
                return scores(row(b), KB, count - b * KB, half, qq)

            def first_pass(b, top):
                return jnp.maximum(top, jnp.max(score(b), axis=0, keepdims=True))

            top = lax.fori_loop(0, nb, first_pass, jnp.zeros((1, 512), F32))

            def second_pass(b, sums):
                p = jnp.exp(score(b) - top)
                dp = dprobs(row(b), KB, half, bb)
                return (
                    sums[0] + jnp.sum(p, axis=0, keepdims=True),
                    sums[1] + jnp.sum(p * dp, axis=0, keepdims=True),
                )

            sums = lax.fori_loop(0, nb, second_pass, (jnp.exp(-top), jnp.zeros((1, 512), F32)))
            inv = 1.0 / sums[0]
            delta = sums[1] * inv

            def third_pass(b, acc):
                weights = jnp.exp(score(b) - top) * inv
                dp = dprobs(row(b), KB, half, bb)
                wb, ds = weights.astype(BF16), (weights * (dp - delta)).astype(BF16)
                attn, dq, dk, dv = products(row(b), KB, half, wb, ds, qq, bb)
                put_keys(row(b), KB, half, dk, dv)
                return acc[0] + attn, acc[1] + dq

            zero = jnp.zeros((GCELLS, 256), F32)
            put(c0, half, *lax.fori_loop(0, nb, third_pass, (zero, zero)))

    def single(g):
        nb = meta_sm[1, g]
        for size in (1, 2, 3):

            @pl.when(nb == size)
            def _():
                at_once((g,), size * KB)

        @pl.when((nb < 1) | (nb > 3))
        def _():
            by_chunks(g)

    def pair(i, carry):
        one, two = 2 * i, 2 * i + 1
        alike = (meta_sm[1, one] == 2) & (meta_sm[1, two] == 2)

        @pl.when(alike)
        def _():
            at_once((one, two), 2 * KB)

        @pl.when(jnp.logical_not(alike))
        def _():
            lax.fori_loop(one, two + 1, lambda g, c: (single(g), c)[1], 0)

        return carry

    lax.fori_loop(0, GROUPS // 2, pair, 0)

    for load in loads[6:]:
        load.wait()
    attn, dq = attn_s[...], dq_s[...]
    outs = []

    def put_out(src, dst):
        outs.append(pltpu.make_async_copy(src, dst, sem_out.at[len(outs)]))
        outs[-1].start()

    upd_v[...] = (lat_v[...].astype(F32) + dot(attn, wo_v[...])).astype(BF16)
    put_out(upd_v, upd_ref)
    dlat_v[...] = (dout_v[...].astype(F32) + dot_nt(dq, wq_v[...])).astype(BF16)
    put_out(dlat_v, dlat_ref)
    main_v[0, 0:512, :] = dot_tn(lat_v[...], dq).astype(BF16)
    main_v[1, 0:512, :] = dot_tn(attn, dout_v[...]).astype(BF16)

    def through_encoder(at):
        return (dot_nt(kv_s[at, :], wkv_v[...]) * slope_s[at, :]).astype(BF16)

    lead = LEAD * KB
    for i in range(lead // SPAN):
        dpre_s[i * SPAN : (i + 1) * SPAN, :] = through_encoder(slice(i * SPAN, (i + 1) * SPAN))

    def lead_kv(i):
        return dot(enct_s[:, 0:lead], kv_s[0:lead, i * 256 : (i + 1) * 256])

    lead_obs = dot(rowst_s[:, 0:lead], dpre_s[...])

    @pl.when(blocks <= LEAD)
    def _():
        for i in range(4):
            main_v[i // 2, 512:1024, i % 2 * 256 : i % 2 * 256 + 256] = lead_kv(i).astype(BF16)
        for h in range(2):
            main_v[h, 1024:1152, :] = lead_obs[h * 128 : (h + 1) * 128].astype(BF16)

    @pl.when(blocks > LEAD)
    def _():
        for i in range(4):
            sums_s[0:512, i * 256 : (i + 1) * 256] = lead_kv(i)
        sums_s[512:768, 0:512] = lead_obs

        def encoder_grads(b, carry):
            at = pl.ds(pl.multiple_of(b * KB, KB), KB)
            sums_s[0:512, :] += dot(enct_s[:, at], kv_s[at, :])
            sums_s[512:768, 0:512] += dot(rowst_s[:, at], through_encoder(at))
            return carry

        lax.fori_loop(LEAD, blocks, encoder_grads, 0)
        for h in range(2):
            main_v[h, 512:1024, :] = sums_s[0:512, h * 512 : (h + 1) * 512].astype(BF16)
            main_v[h, 1024:1152, :] = sums_s[512 + h * 128 : 640 + h * 128, 0:512].astype(BF16)

    put_out(main_v, main_ref)
    for out in outs:
        out.wait()


ORDER = ("x", "y", "z")
JOBS = ((0, 384, 0), (384, 384, 1), (768, 384, 2))
HALF = 1152


def peer(step_axis, k):
    lat, lon = lax.axis_index("lat"), lax.axis_index("lon")
    y, core, z, x = lat // 2, lat % 2, lon // 4, lon % 4
    if step_axis == "x":
        x = (x + k) % 4
    elif step_axis == "y":
        y = (y + k) % 4
    elif step_axis == "z":
        z = (z + k) % 4
    else:
        core = 1 - core
    return {"lat": y * 2 + core, "lon": z * 4 + x}


def place_on(step_axis):
    lat, lon = lax.axis_index("lat"), lax.axis_index("lon")
    return {"x": lon % 4, "y": lat // 2, "z": lon // 4}[step_axis]


class Job:
    def __init__(self, far, near, out, half, start, rows, turn, bufs, sems):
        self.far, self.near, self.start, self.rows, self.piece = far, near, start, rows, rows // 4
        self.axes = [ORDER[(turn + i) % 3] for i in range(3)]
        self.core_recv, self.src1, self.recv1, self.src2, self.recv2, self.buf3 = bufs
        self.sems, self.half, self.phase, self.sent = sems, half, -1, []
        self.result = out.at[half, pl.ds(start, rows), :]

    def describe(self, src, dst, axis, k):
        return pltpu.make_async_remote_copy(
            src_ref=src, dst_ref=dst, send_sem=self.sems.at[self.phase, 0], recv_sem=self.sems.at[self.phase, 1],
            device_id=peer(axis, k), device_id_type=MESH,
        )

    def across(self, src, dst):
        self.phase += 1
        copy = self.describe(src, dst, "core", 1)
        copy.start()
        self.sent.append(copy)

    def around(self, axis, src_of, dst_of, whole):
        self.phase += 1
        for k in range(1, 4):
            self.describe(src_of(k), dst_of(k), axis, k).start()
        self.sent.append(self.describe(whole, whole, axis, 1))

    def arrived(self):
        self.sent[-1].wait_recv()

    def swap(self):
        self.across(self.far.at[1 - self.half, pl.ds(self.start, self.rows), :], self.core_recv)

    def scatter1(self):
        self.arrived()
        own = self.near[self.half, self.start : self.start + self.rows, :].astype(F32)
        total = (own + self.core_recv[...].astype(F32)).astype(BF16)
        for j in range(4):
            self.src1[j] = total[j * self.piece : (j + 1) * self.piece, :]
        at = place_on(self.axes[0])
        self.around(
            self.axes[0], lambda k: self.src1.at[lax.rem(at + k, 4)], lambda k: self.recv1.at[k - 1], self.recv1
        )

    def scatter2(self):
        self.arrived()
        total = self.src1[place_on(self.axes[0])].astype(F32)
        for k in range(3):
            total = total + self.recv1[k].astype(F32)
        for j in range(4):
            self.src2[j] = total[:, j * 128 : (j + 1) * 128].astype(BF16)
        at = place_on(self.axes[1])
        self.around(
            self.axes[1], lambda k: self.src2.at[lax.rem(at + k, 4)], lambda k: self.recv2.at[k - 1], self.recv2
        )

    def exchange3(self):
        self.arrived()
        total = self.src2[place_on(self.axes[1])].astype(F32)
        for k in range(3):
            total = total + self.recv2[k].astype(F32)
        self.buf3[0] = total.astype(BF16)
        self.around(self.axes[2], lambda k: self.buf3.at[0], lambda k: self.buf3.at[k], self.buf3.at[1:4])

    def gather2(self):
        self.arrived()
        at = place_on(self.axes[2])
        total = self.buf3[at].astype(F32)
        for s in range(1, 4):
            total = total + self.buf3[lax.rem(at + 4 - s, 4)].astype(F32)
        rows = pl.ds(pl.multiple_of(place_on(self.axes[0]) * self.piece, self.piece), self.piece)
        lanes = pl.ds(pl.multiple_of(place_on(self.axes[1]) * 128, 128), 128)
        self.result[rows, lanes] = total.astype(BF16)
        mine = self.result.at[rows, lanes]
        self.around(self.axes[1], lambda k: mine, lambda k: mine, self.recv2)

    def gather1(self):
        self.arrived()
        mine = self.result.at[pl.ds(pl.multiple_of(place_on(self.axes[0]) * self.piece, self.piece), self.piece), :]
        self.around(self.axes[0], lambda k: mine, lambda k: mine, self.recv1)

    def share(self):
        self.arrived()
        self.across(self.result, self.result)

    def settle(self):
        for copy in self.sent:
            copy.wait_send()


def sum_kernel(main_ref, out_ref, main_v, out_v, sem_in, sem_out, *scratch):
    half = lax.rem(lax.axis_index("lat"), 2)
    load = pltpu.make_async_copy(main_ref.at[half], main_v.at[half], sem_in)
    load.start()
    barrier = pltpu.get_barrier_semaphore()
    pl.semaphore_signal(barrier, inc=1, device_id=peer("core", 1), device_id_type=MESH)
    for axis in ORDER:
        for k in range(1, 4):
            pl.semaphore_signal(barrier, inc=1, device_id=peer(axis, k), device_id_type=MESH)
    jobs = []
    for i, (start, rows, turn) in enumerate(JOBS):
        jobs.append(Job(main_ref, main_v, out_v, half, start, rows, turn, scratch[7 * i : 7 * i + 6], scratch[7 * i + 6]))
    stores = []

    def store(job, i, h):
        at = pl.ds(job.start, job.rows)
        stores.append(pltpu.make_async_copy(out_v.at[h, at, :], out_ref.at[h, at, :], sem_out.at[i]))
        stores[-1].start()

    pl.semaphore_wait(barrier, 10)
    for job in jobs:
        job.swap()
    load.wait()
    for what in ("scatter1", "scatter2", "exchange3", "gather2", "gather1"):
        for job in jobs:
            getattr(job, what)()
    for i, job in enumerate(jobs):
        job.share()
        store(job, i, half)
    for i, job in enumerate(jobs):
        job.arrived()
        store(job, 3 + i, 1 - half)
    for job in jobs:
        job.settle()
    for copy in stores:
        copy.wait()


def widen_kernel(gobs_ref, gkv_ref, gqo_ref, obs_ref, kv_ref, q_ref, o_ref):
    obs_ref[...] = gobs_ref[0].astype(F32)
    q_ref[...] = gqo_ref[0].astype(F32)
    o_ref[...] = gqo_ref[1].astype(F32)
    for h in range(2):
        kv_ref[:, h * D : (h + 1) * D] = gkv_ref[h].astype(F32)


def sum_grads(main):
    far = pl.BlockSpec(memory_space=pltpu.HBM)
    dma = pltpu.SemaphoreType.DMA
    scratch = []
    for _, n, _ in JOBS:
        piece = n // 4
        scratch += [
            pltpu.VMEM((n, D), BF16),
            pltpu.VMEM((4, piece, D), BF16),
            pltpu.VMEM((3, piece, D), BF16),
            pltpu.VMEM((4, piece, 128), BF16),
            pltpu.VMEM((3, piece, 128), BF16),
            pltpu.VMEM((4, piece, 128), BF16),
            dma((7, 2)),
        ]
    return pl.pallas_call(
        sum_kernel,
        out_shape=jax.ShapeDtypeStruct((2, HALF, D), BF16),
        in_specs=[far],
        out_specs=far,
        scratch_shapes=[
            pltpu.VMEM((2, HALF, D), BF16),
            pltpu.VMEM((2, HALF, D), BF16),
            dma,
            dma((6,)),
        ] + scratch,
        compiler_params=pltpu.CompilerParams(
            collective_id=1, has_side_effects=True, vmem_limit_bytes=VMEM_LIMIT
        ),
        name="sum_grads",
    )(main)


def body(latents, d_out, observations, obs_bias, footprint, obs_cell, w_obs, w_kv, w_q, w_o):
    vmem = pl.BlockSpec(memory_space=pltpu.VMEM)
    dma = pltpu.SemaphoreType.DMA
    far = pl.BlockSpec(memory_space=pltpu.HBM)
    recv, rmeta, q, back = pl.pallas_call(
        exchange_kernel,
        out_shape=(
            jax.ShapeDtypeStruct((2, 64, 16, CH), BF16),
            jax.ShapeDtypeStruct((2, 64, 1, 128), F32),
            jax.ShapeDtypeStruct((CELLS, D), BF16),
            jax.ShapeDtypeStruct((CELLS, D), BF16),
        ),
        in_specs=[far] * 8,
        out_specs=[far] * 4,
        scratch_shapes=[
            pltpu.VMEM((4, 32), jnp.int32),
            pltpu.VMEM((32 * OBS, CH), BF16),
            pltpu.VMEM((OBS, 32), BF16),
            pltpu.VMEM((4, OBS, 32), jnp.int32),
            pltpu.VMEM((CELLS, D), BF16),
            pltpu.VMEM((CELLS, D), BF16),
            pltpu.VMEM((D, D), BF16),
            pltpu.VMEM((D, D), BF16),
            pltpu.VMEM((CELLS, D), BF16),
            pltpu.VMEM((CELLS, D), BF16),
            pltpu.VMEM((2, 64, 16, CH), BF16),
            pltpu.VMEM((2, 64, 1, 128), F32),
            pltpu.VMEM((64, 16, CH), BF16),
            pltpu.VMEM((64, 1, 128), F32),
            pltpu.VMEM((16, 128), F32),
            pltpu.VMEM((128, 1280), F32),
            dma((8,)),
            dma((4,)),
            dma((2, 2)),
            dma((2, 2)),
        ],
        compiler_params=pltpu.CompilerParams(
            collective_id=0, has_side_effects=True, vmem_limit_bytes=VMEM_LIMIT
        ),
        name="exchange",
    )(
        footprint.T, observations.reshape(-1, CH), obs_bias.T, obs_cell.transpose(1, 2, 0),
        latents, d_out, w_q, w_o,
    )
    upd, dlat, main = pl.pallas_call(
        tile_kernel,
        out_shape=(
            jax.ShapeDtypeStruct((CELLS, D), BF16),
            jax.ShapeDtypeStruct((CELLS, D), BF16),
            jax.ShapeDtypeStruct((2, HALF, D), BF16),
        ),
        in_specs=[far] * 10,
        out_specs=[far] * 3,
        scratch_shapes=[
            pltpu.VMEM((CH, MAXB * KB), BF16),
            pltpu.VMEM((MAXB * KB, D), F32),
            pltpu.VMEM((D, MAXB * KB), BF16),
            pltpu.VMEM((MAXB * KB, 2 * D), BF16),
            pltpu.VMEM((MAXB * KB, 128), F32),
            pltpu.VMEM((CELLS, D), BF16),
            pltpu.VMEM((CELLS, D), BF16),
            pltpu.VMEM((LEAD * KB, D), BF16),
            pltpu.VMEM((768, 2 * D), F32),
            pltpu.VMEM((2, HALF, D), BF16),
            pltpu.VMEM((CELLS, D), BF16),
            pltpu.VMEM((CELLS, D), BF16),
            pltpu.SMEM((3, GROUPS), jnp.int32),
            pltpu.VMEM((ROWS, CH), BF16),
            pltpu.VMEM((DEV, 128), F32),
            pltpu.VMEM((CELLS, D), BF16),
            pltpu.VMEM((CELLS, D), BF16),
            pltpu.VMEM((CELLS, D), BF16),
            pltpu.VMEM((CELLS, D), BF16),
            pltpu.VMEM((CH, D), BF16),
            pltpu.VMEM((D, 2 * D), BF16),
            pltpu.VMEM((D, D), BF16),
            pltpu.VMEM((D, D), BF16),
            dma((10,)),
            dma((3,)),
        ],
        compiler_params=pltpu.CompilerParams(vmem_limit_bytes=VMEM_LIMIT),
        name="tile",
    )(recv.reshape(ROWS, CH), rmeta.reshape(DEV, 128), q, back, latents, d_out, w_obs, w_kv, w_q, w_o)
    total = sum_grads(main)
    gobs, gkv, gq, go = pl.pallas_call(
        widen_kernel,
        grid=(4,),
        out_shape=[jax.ShapeDtypeStruct(x.shape, F32) for x in (w_obs, w_kv, w_q, w_o)],
        in_specs=[
            pl.BlockSpec((1, 64, D), lambda i: (i // 2, 16 + i % 2, 0)),
            pl.BlockSpec((2, 128, D), lambda i: (0, 4 + i, 0)),
            pl.BlockSpec((2, 128, D), lambda i: (0, i, 0)),
        ],
        out_specs=[
            pl.BlockSpec((64, D), lambda i: (i, 0)),
            pl.BlockSpec((128, 2 * D), lambda i: (i, 0)),
            pl.BlockSpec((128, D), lambda i: (i, 0)),
            pl.BlockSpec((128, D), lambda i: (i, 0)),
        ],
        compiler_params=pltpu.CompilerParams(vmem_limit_bytes=VMEM_LIMIT),
        name="widen",
    )(total, total, total)
    return upd, dlat, gobs, gkv, gq, go


def solution(mesh):
    spread = ("lat", "lon")
    placed = (
        P(spread, None), P(spread, None), P(spread, None, None), P(spread, None), P(spread, None),
        P(spread, None, None), P(), P(), P(), P(),
    )
    return jax.shard_map(
        body,
        mesh=mesh,
        in_specs=placed,
        out_specs=(P(spread, None), P(spread, None), P(), P(), P(), P()),
        check_vma=False,
    )
```

```python
import functools
import math

import jax
import jax.numpy as jnp
from jax import lax
from jax.experimental import pallas as pl
from jax.experimental.pallas import tpu as pltpu
from jax.sharding import PartitionSpec as P

HEADS = 8
GROUPS = 8
DEV = 128
OBS = 8
CAP = 2
CH = 256
D = 512
CELLS = 1024
GCELLS = CELLS // GROUPS
ROWS = DEV * CAP * OBS
KB = 128
MAXB = 24
LEAD = 18
SPAN = 768
F32 = jnp.float32
BF16 = jnp.bfloat16
NEG = -1e30
VMEM_LIMIT = 59 << 20
MESH = pl.DeviceIdType.MESH


def dot(a, b):
    return lax.dot_general(a, b, (((1,), (0,)), ((), ())), preferred_element_type=F32)


def dot_nt(a, b):
    return lax.dot_general(a, b, (((1,), (1,)), ((), ())), preferred_element_type=F32)


def dot_tn(a, b):
    return lax.dot_general(a, b, (((0,), (0,)), ((), ())), preferred_element_type=F32)


def iota(shape, dim):
    return lax.broadcasted_iota(jnp.int32, shape, dim)


def gelu_parts(x):
    a = jnp.abs(x)
    t = 1.0 / (1.0 + (0.3275911 / math.sqrt(2.0)) * a)
    e = jnp.exp(-0.5 * x * x)
    poly = t * (
        0.5 * 0.254829592
        + t * (-0.5 * 0.284496736 + t * (0.5 * 1.421413741 + t * (-0.5 * 1.453152027 + t * (0.5 * 1.061405429))))
    )
    tail = poly * e
    cdf = jnp.where(x < 0.0, tail, 1.0 - tail)
    return x * cdf, cdf + x * e * (1.0 / math.sqrt(2.0 * math.pi))


def hot(mask):
    return jnp.where(mask, 1.0, 0.0).astype(BF16)


def exchange_kernel(
    foot_ref, obs_ref, bias_ref, cell_ref, lat_ref, dout_ref, wq_ref, wo_ref,
    recv_ref, rmeta_ref, q_ref, back_ref,
    foot_v, obs_v, bias_v, cell_v, lat_v, dout_v, wq_v, wo_v, q_v, back_v,
    stage, mstage, osend, omsend, foot_s, marks_s, sem_in, sem_out, sem_core, sem_chip,
):
    lat, lon = lax.axis_index("lat"), lax.axis_index("lon")
    core = lax.rem(lat, 2)
    y, z, x = lat // 2, lon // 4, lax.rem(lon, 4)
    loads = []
    for i, (src, dst) in enumerate((
        (foot_ref, foot_v), (obs_ref, obs_v), (bias_ref, bias_v), (cell_ref, cell_v),
        (lat_ref, lat_v), (wq_ref, wq_v), (dout_ref, dout_v), (wo_ref, wo_v),
    )):
        loads.append(pltpu.make_async_copy(src, dst, sem_in.at[i]))
        loads[-1].start()

    ys = [lax.rem(y + d, 4) for d in range(4)]
    lons = [lax.rem(z + d // 4, 4) * 4 + lax.rem(x + d % 4, 4) for d in range(16)]
    chips = []
    for k in range(1, 64):
        cy, cl = ys[k // 16], lons[k % 16]
        chips.append((cy * 16 + cl, {"lat": cy * 2 + core, "lon": cl}))
    sibling = {"lat": y * 2 + 1 - core, "lon": lon}
    my_chip = y * 16 + lon
    barrier = pltpu.get_barrier_semaphore()
    pl.semaphore_signal(barrier, inc=1, device_id=sibling, device_id_type=MESH)
    for chip, where in chips:
        pl.semaphore_signal(barrier, inc=1, device_id=where, device_id_type=MESH)

    foot_s[...] = jnp.full((16, 128), -1.0, F32)
    marks_s[...] = jnp.zeros((128, 1280), F32)
    for load in loads[:4]:
        load.wait()
    foot_s[0:4, 0:32] = foot_v[...].astype(F32)
    for rank in range(CAP):
        lane, at = rank * OBS, rank * 640
        marks_s[lane : lane + OBS, at : at + 32] = bias_v[...].astype(F32)
        for f in range(4):
            lane, at = (CAP + rank) * OBS, rank * 640 + (1 + f) * 128
            marks_s[lane : lane + OBS, at : at + 32] = cell_v[f].astype(F32) - float(GROUPS)
    foot = foot_s[...]
    marks = marks_s[...].astype(BF16)
    r, c = iota((128, 128), 0), iota((128, 128), 1)
    upper = hot(r < c)
    widen = hot(iota((128, 256), 1) // OBS == iota((128, 256), 0))
    keep = iota((1024, 256), 0) % OBS == iota((1024, 256), 1) % OBS

    def slots_of(to_core):
        tile = (r // 32) * 32 + to_core * 16 + (r // CAP) % 16
        hit = jnp.zeros((128, 128), F32)
        for f in range(4):
            hit = hit + jnp.where(foot[f : f + 1, :] == tile.astype(F32), 1.0, 0.0)
        sel = hit * jnp.where(dot(hit.astype(BF16), upper) == (r % CAP).astype(F32), 1.0, 0.0)
        blocks = dot(sel.astype(BF16), widen)
        spread = jnp.broadcast_to(blocks[:, None, :], (128, OBS, 256)).reshape(1024, 256)
        rows = dot(jnp.where(keep, spread, 0.0).astype(BF16), obs_v[...]).astype(BF16)
        tile = iota((64, 128), 0)
        tile = ((tile // 16) * 32 + to_core * 16 + tile % 16).astype(F32)
        hits = [jnp.where(foot[f : f + 1, :] == tile, 1.0, 0.0) for f in range(4)]
        any_hit = hits[0] + hits[1] + hits[2] + hits[3]
        order = dot(any_hit.astype(BF16), upper)
        left = []
        for rank in range(CAP):
            chosen = any_hit * jnp.where(order == float(rank), 1.0, 0.0)
            left += [chosen] + [chosen * hits[f] for f in range(4)]
        meta = dot_nt(jnp.concatenate(left, axis=1).astype(BF16), marks)
        return rows.reshape(64, 16, CH), meta.reshape(64, 1, 128)

    osend[...], omsend[...] = slots_of(1 - core)
    stage[core], mstage[core] = slots_of(core)
    pl.semaphore_wait(barrier, 64)

    def copy(src, dst, sems, where):
        return pltpu.make_async_remote_copy(
            src_ref=src, dst_ref=dst, send_sem=sems.at[0], recv_sem=sems.at[1], device_id=where, device_id_type=MESH,
        )

    swap = [copy(osend, stage.at[core], sem_core.at[0], sibling), copy(omsend, mstage.at[core], sem_core.at[1], sibling)]
    for part in swap:
        part.start()
    for chip, where in chips:
        copy(stage.at[core, chip], recv_ref.at[core, my_chip], sem_chip.at[0], where).start()
    for part in swap:
        part.wait_recv()
    for chip, where in chips:
        copy(stage.at[1 - core, chip], recv_ref.at[1 - core, my_chip], sem_chip.at[1], where).start()
        copy(mstage.at[:, chip], rmeta_ref.at[:, my_chip], sem_chip.at[2], where).start()
    stores = [
        pltpu.make_async_copy(stage.at[:, my_chip], recv_ref.at[:, my_chip], sem_out.at[0]),
        pltpu.make_async_copy(mstage.at[:, my_chip], rmeta_ref.at[:, my_chip], sem_out.at[1]),
    ]
    for store in stores:
        store.start()

    loads[4].wait()
    loads[5].wait()
    q_v[...] = (dot(lat_v[...], wq_v[...]).astype(BF16).astype(F32) * 0.125).astype(BF16)
    stores.append(pltpu.make_async_copy(q_v, q_ref, sem_out.at[2]))
    stores[-1].start()
    loads[6].wait()
    loads[7].wait()
    back_v[...] = dot_nt(dout_v[...], wo_v[...]).astype(BF16)
    stores.append(pltpu.make_async_copy(back_v, back_ref, sem_out.at[3]))
    stores[-1].start()

    whole = [
        copy(stage.at[core, 0:63], recv_ref.at[core, 0:63], sem_chip.at[0], sibling),
        copy(stage.at[1 - core, 0:63], recv_ref.at[1 - core, 0:63], sem_chip.at[1], sibling),
        copy(mstage.at[:, 0:63], rmeta_ref.at[:, 0:63], sem_chip.at[2], sibling),
    ]
    for part in whole:
        part.wait_recv()
    for part in whole:
        part.wait_send()
    for part in swap:
        part.wait_send()
    for store in stores:
        store.wait()


def tile_kernel(
    recv_ref, rmeta_ref, q_ref, back_ref, lat_ref, dout_ref, wobs_ref, wkv_ref, wq_ref, wo_ref,
    upd_ref, dlat_ref, main_ref,
    rowst_s, slope_s, enct_s, kv_s, bias_s, attn_s, dq_s, dpre_s, sums_s, main_v, upd_v, dlat_v, meta_sm,
    recv_v, rmeta_v, q_s, back_s, lat_v, dout_v, wobs_v, wkv_v, wq_v, wo_v, sem_in, sem_out,
):
    loads = []
    for i, (src, dst) in enumerate((
        (rmeta_ref, rmeta_v), (recv_ref, recv_v), (wobs_ref, wobs_v), (wkv_ref, wkv_v), (q_ref, q_s), (back_ref, back_s),
        (lat_ref, lat_v), (dout_ref, dout_v), (wq_ref, wq_v), (wo_ref, wo_v),
    )):
        loads.append(pltpu.make_async_copy(src, dst, sem_in.at[i]))
        loads[-1].start()

    loads[0].wait()
    r, c = iota((128, 128), 0), iota((128, 128), 1)
    marks = rmeta_v[...].astype(BF16)
    own_lane = r % 8 == c // 16
    chunk = jnp.where(iota((16, 128), 0) == iota((16, 128), 1) // 8, 1.0, 0.0).astype(BF16)

    def laned(first_lane):
        lanes = dot(marks, jnp.where(r == c % 16 + first_lane, 1.0, 0.0).astype(BF16))
        return dot(chunk, jnp.where(own_lane, lanes, 0.0).astype(BF16))

    bias_row = laned(0)
    cell = laned(16) + float(GROUPS)
    inside = jnp.concatenate([jnp.where(cell == float(g), 1.0, 0.0) for g in range(GROUPS)], axis=0)
    upto = jnp.where(r <= c, 1.0, 0.0).astype(BF16)
    prefix = dot(inside.astype(BF16), upto)
    total = jnp.broadcast_to(prefix[:, 127:128], (128, 128)).astype(BF16)
    same = r // 16 == c // 16
    before = dot(jnp.where(same & (c < r), 1.0, 0.0).astype(BF16), total)
    count = dot(jnp.where(same, 1.0, 0.0).astype(BF16), total)
    nblk = jnp.floor((count + (KB - 1.0)) * (1.0 / KB))
    first = dot(jnp.where((c % 16 == 0) & (c // 16 < r // 16), 1.0, 0.0).astype(BF16), nblk.astype(BF16))
    place = jnp.where(inside > 0.5, first * float(KB) + before + prefix - 1.0, -1.0)
    pos = place[0:16, :]
    for g in range(1, GROUPS):
        pos = jnp.maximum(pos, place[g * 16 : (g + 1) * 16, :])
    for g in range(GROUPS):
        meta_sm[0, g] = jnp.max(first[g * 16 : g * 16 + 8, :]).astype(jnp.int32)
        meta_sm[1, g] = jnp.max(nblk[g * 16 : g * 16 + 8, :]).astype(jnp.int32)
        meta_sm[2, g] = jnp.max(count[g * 16 : g * 16 + 8, :]).astype(jnp.int32)
    blocks = meta_sm[0, GROUPS - 1] + meta_sm[1, GROUPS - 1]

    lane_pos = [jnp.broadcast_to(pos[i : i + 1, :], (16, 128)) for i in range(16)]
    lane_bias = [jnp.broadcast_to(bias_row[i : i + 1, :], (16, 128)).astype(BF16) for i in range(16)]
    row_id = iota((256, 128), 0).astype(F32).astype(BF16)

    def gather(base, rows):
        cols = []
        bias = jnp.zeros((rows, 128), BF16)
        for i in range(16):
            rel = jnp.clip(lane_pos[i] - base, -1.0, float(rows)).astype(BF16)
            found = row_id[0:rows] == jnp.concatenate([rel] * (rows // 16), axis=0)
            cols.append(jnp.where(found, jnp.ones((), BF16), jnp.zeros((), BF16)))
            bias = jnp.where(found, jnp.concatenate([lane_bias[i]] * (rows // 16), axis=0), bias)
        bias = jnp.sum(bias.astype(F32), axis=1, keepdims=True)
        return jnp.concatenate(cols, axis=1), jnp.broadcast_to(bias, (rows, 128))

    def picked(at, picks):
        bias_s[at, :] = jnp.concatenate([pick[1] for pick in picks], axis=0)
        rows = dot(jnp.concatenate([pick[0] for pick in picks], axis=0), recv_v[...]).astype(BF16)
        rowst_s[:, at] = rows.T
        return dot(rows, wobs_v[...])

    def encoded(at, pre):
        value, slope = gelu_parts(pre)
        enc = value.astype(BF16)
        slope_s[at, :] = slope
        enct_s[:, at] = enc.T
        kv_s[at, :] = dot(enc, wkv_v[...]).astype(BF16)

    for load in loads[1:4]:
        load.wait()
    last = None
    for i in range(LEAD * KB // SPAN):
        at = slice(i * SPAN, (i + 1) * SPAN)
        pre = picked(at, [gather(float(i * SPAN + j), 256) for j in range(0, SPAN, 256)])
        if last is not None:
            encoded(*last)
        last = (at, pre)
    encoded(*last)

    def encode(b, carry):
        at = pl.ds(pl.multiple_of(b * KB, KB), KB)
        encoded(at, picked(at, [gather((b * KB).astype(F32), KB)]))
        return carry

    lax.fori_loop(LEAD, blocks, encode, 0)
    for load in loads[4:6]:
        load.wait()

    lane_head = iota((GCELLS, 256), 1) // 64

    def spread_heads(x):
        return jnp.concatenate([jnp.where(lane_head == h, x, jnp.zeros((), BF16)) for h in range(4)], axis=0)

    def scores(r0, rows, valid, half, qq):
        keys = kv_s[pl.ds(r0, rows), half * 256 : half * 256 + 256]
        bias = jnp.where(iota((rows, 128), 0) < valid, bias_s[pl.ds(r0, rows), :], NEG)
        return dot_nt(keys, qq) + jnp.concatenate([bias] * 4, axis=1)

    def dprobs(r0, rows, half, bb):
        return dot_nt(kv_s[pl.ds(r0, rows), D + half * 256 : D + half * 256 + 256], bb)

    def diagonal(x):
        out = x[0:GCELLS]
        for h in range(1, 4):
            out = jnp.where(lane_head == h, x[h * GCELLS : (h + 1) * GCELLS], out)
        return out

    def products(r0, rows, half, wb, ds, qq, bb):
        keys = kv_s[pl.ds(r0, rows), half * 256 : half * 256 + 256]
        values = kv_s[pl.ds(r0, rows), D + half * 256 : D + half * 256 + 256]
        attn = diagonal(dot(wb.T, values))
        dq = diagonal(dot(ds.T, keys))
        return attn, dq, dot(ds, qq).astype(BF16), dot(wb, bb).astype(BF16)

    def put_keys(r0, rows, half, dk, dv):
        kv_s[pl.ds(r0, rows), half * 256 : half * 256 + 256] = dk
        kv_s[pl.ds(r0, rows), D + half * 256 : D + half * 256 + 256] = dv

    def heads(c0, half):
        lanes = slice(half * 256, half * 256 + 256)
        return spread_heads(q_s[pl.ds(c0, GCELLS), lanes]), spread_heads(back_s[pl.ds(c0, GCELLS), lanes])

    def put(c0, half, attn, dq):
        lanes = slice(half * 256, half * 256 + 256)
        attn_s[pl.ds(c0, GCELLS), lanes] = attn.astype(BF16)
        dq_s[pl.ds(c0, GCELLS), lanes] = (dq * 0.125).astype(BF16)

    def at_once(groups, rows):
        jobs = []
        for g in groups:
            r0, c0 = pl.multiple_of(meta_sm[0, g] * KB, KB), pl.multiple_of(g * GCELLS, GCELLS)
            for half in range(2):
                jobs.append((r0, c0, half, meta_sm[2, g]) + heads(c0, half))
        raw = [scores(r0, rows, valid, half, qq) for r0, _, half, valid, qq, _ in jobs]
        dps = [dprobs(r0, rows, half, bb) for r0, _, half, _, _, bb in jobs]
        done = []
        for (r0, _, half, _, qq, bb), s, dp in zip(jobs, raw, dps):
            top = jnp.maximum(jnp.max(s, axis=0, keepdims=True), 0.0)
            p = jnp.exp(s - top)
            inv = 1.0 / (jnp.exp(-top) + jnp.sum(p, axis=0, keepdims=True))
            weights = p * inv
            delta = jnp.sum(weights * dp, axis=0, keepdims=True)
            wb, ds = weights.astype(BF16), (weights * (dp - delta)).astype(BF16)
            done.append(products(r0, rows, half, wb, ds, qq, bb))
        for (r0, c0, half, _, _, _), (attn, dq, dk, dv) in zip(jobs, done):
            put_keys(r0, rows, half, dk, dv)
            put(c0, half, attn, dq)

    def by_chunks(g):
        start, nb, count = meta_sm[0, g], meta_sm[1, g], meta_sm[2, g]
        c0 = pl.multiple_of(g * GCELLS, GCELLS)
        for half in range(2):
            qq, bb = heads(c0, half)

            def row(b):
                return pl.multiple_of((start + b) * KB, KB)

            def score(b):
                return scores(row(b), KB, count - b * KB, half, qq)

            def first_pass(b, top):
                return jnp.maximum(top, jnp.max(score(b), axis=0, keepdims=True))

            top = lax.fori_loop(0, nb, first_pass, jnp.zeros((1, 512), F32))

            def second_pass(b, sums):
                p = jnp.exp(score(b) - top)
                dp = dprobs(row(b), KB, half, bb)
                return (
                    sums[0] + jnp.sum(p, axis=0, keepdims=True),
                    sums[1] + jnp.sum(p * dp, axis=0, keepdims=True),
                )

            sums = lax.fori_loop(0, nb, second_pass, (jnp.exp(-top), jnp.zeros((1, 512), F32)))
            inv = 1.0 / sums[0]
            delta = sums[1] * inv

            def third_pass(b, acc):
                weights = jnp.exp(score(b) - top) * inv
                dp = dprobs(row(b), KB, half, bb)
                wb, ds = weights.astype(BF16), (weights * (dp - delta)).astype(BF16)
                attn, dq, dk, dv = products(row(b), KB, half, wb, ds, qq, bb)
                put_keys(row(b), KB, half, dk, dv)
                return acc[0] + attn, acc[1] + dq

            zero = jnp.zeros((GCELLS, 256), F32)
            put(c0, half, *lax.fori_loop(0, nb, third_pass, (zero, zero)))

    def single(g):
        nb = meta_sm[1, g]
        for size in (1, 2, 3):

            @pl.when(nb == size)
            def _():
                at_once((g,), size * KB)

        @pl.when((nb < 1) | (nb > 3))
        def _():
            by_chunks(g)

    def pair(i, carry):
        one, two = 2 * i, 2 * i + 1
        alike = (meta_sm[1, one] == 2) & (meta_sm[1, two] == 2)

        @pl.when(alike)
        def _():
            at_once((one, two), 2 * KB)

        @pl.when(jnp.logical_not(alike))
        def _():
            lax.fori_loop(one, two + 1, lambda g, c: (single(g), c)[1], 0)

        return carry

    lax.fori_loop(0, GROUPS // 2, pair, 0)

    for load in loads[6:]:
        load.wait()
    attn, dq = attn_s[...], dq_s[...]
    outs = []

    def put_out(src, dst):
        outs.append(pltpu.make_async_copy(src, dst, sem_out.at[len(outs)]))
        outs[-1].start()

    upd_v[...] = (lat_v[...].astype(F32) + dot(attn, wo_v[...])).astype(BF16)
    put_out(upd_v, upd_ref)
    dlat_v[...] = (dout_v[...].astype(F32) + dot_nt(dq, wq_v[...])).astype(BF16)
    put_out(dlat_v, dlat_ref)
    main_v[0, 0:512, :] = dot_tn(lat_v[...], dq).astype(BF16)
    main_v[1, 0:512, :] = dot_tn(attn, dout_v[...]).astype(BF16)

    def through_encoder(at):
        return (dot_nt(kv_s[at, :], wkv_v[...]) * slope_s[at, :]).astype(BF16)

    lead = LEAD * KB
    for i in range(lead // SPAN):
        dpre_s[i * SPAN : (i + 1) * SPAN, :] = through_encoder(slice(i * SPAN, (i + 1) * SPAN))

    def lead_kv(i):
        return dot(enct_s[:, 0:lead], kv_s[0:lead, i * 256 : (i + 1) * 256])

    lead_obs = dot(rowst_s[:, 0:lead], dpre_s[...])

    @pl.when(blocks <= LEAD)
    def _():
        for i in range(4):
            main_v[i // 2, 512:1024, i % 2 * 256 : i % 2 * 256 + 256] = lead_kv(i).astype(BF16)
        for h in range(2):
            main_v[h, 1024:1152, :] = lead_obs[h * 128 : (h + 1) * 128].astype(BF16)

    @pl.when(blocks > LEAD)
    def _():
        for i in range(4):
            sums_s[0:512, i * 256 : (i + 1) * 256] = lead_kv(i)
        sums_s[512:768, 0:512] = lead_obs

        def encoder_grads(b, carry):
            at = pl.ds(pl.multiple_of(b * KB, KB), KB)
            sums_s[0:512, :] += dot(enct_s[:, at], kv_s[at, :])
            sums_s[512:768, 0:512] += dot(rowst_s[:, at], through_encoder(at))
            return carry

        lax.fori_loop(LEAD, blocks, encoder_grads, 0)
        for h in range(2):
            main_v[h, 512:1024, :] = sums_s[0:512, h * 512 : (h + 1) * 512].astype(BF16)
            main_v[h, 1024:1152, :] = sums_s[512 + h * 128 : 640 + h * 128, 0:512].astype(BF16)

    put_out(main_v, main_ref)
    for out in outs:
        out.wait()


ORDER = ("x", "y", "z")
JOBS = tuple((i * 128, 128, i % 3) for i in range(9))
HALF = 1152


def peer(step_axis, k):
    lat, lon = lax.axis_index("lat"), lax.axis_index("lon")
    y, core, z, x = lat // 2, lat % 2, lon // 4, lon % 4
    if step_axis == "x":
        x = (x + k) % 4
    elif step_axis == "y":
        y = (y + k) % 4
    elif step_axis == "z":
        z = (z + k) % 4
    else:
        core = 1 - core
    return {"lat": y * 2 + core, "lon": z * 4 + x}


def place_on(step_axis):
    lat, lon = lax.axis_index("lat"), lax.axis_index("lon")
    return {"x": lon % 4, "y": lat // 2, "z": lon // 4}[step_axis]


class Job:
    def __init__(self, far, near, out, half, start, rows, turn, bufs, sems):
        self.far, self.near, self.start, self.rows, self.piece = far, near, start, rows, rows // 4
        self.axes = [ORDER[(turn + i) % 3] for i in range(3)]
        self.core_recv, self.src1, self.recv1, self.src2, self.recv2, self.buf3 = bufs
        self.sems, self.half, self.phase, self.sent = sems, half, -1, []
        self.result = out.at[half, pl.ds(start, rows), :]

    def describe(self, src, dst, axis, k):
        return pltpu.make_async_remote_copy(
            src_ref=src, dst_ref=dst, send_sem=self.sems.at[self.phase, 0], recv_sem=self.sems.at[self.phase, 1],
            device_id=peer(axis, k), device_id_type=MESH,
        )

    def across(self, src, dst):
        self.phase += 1
        copy = self.describe(src, dst, "core", 1)
        copy.start()
        self.sent.append(copy)

    def around(self, axis, src_of, dst_of, whole):
        self.phase += 1
        for k in range(1, 4):
            self.describe(src_of(k), dst_of(k), axis, k).start()
        self.sent.append(self.describe(whole, whole, axis, 1))

    def arrived(self):
        self.sent[-1].wait_recv()

    def swap(self):
        self.across(self.far.at[1 - self.half, pl.ds(self.start, self.rows), :], self.core_recv)

    def scatter1(self):
        self.arrived()
        own = self.near[self.half, self.start : self.start + self.rows, :].astype(F32)
        total = (own + self.core_recv[...].astype(F32)).astype(BF16)
        for j in range(4):
            self.src1[j] = total[j * self.piece : (j + 1) * self.piece, :]
        at = place_on(self.axes[0])
        self.around(
            self.axes[0], lambda k: self.src1.at[lax.rem(at + k, 4)], lambda k: self.recv1.at[k - 1], self.recv1
        )

    def scatter2(self):
        self.arrived()
        total = self.src1[place_on(self.axes[0])].astype(F32)
        for k in range(3):
            total = total + self.recv1[k].astype(F32)
        for j in range(4):
            self.src2[j] = total[:, j * 128 : (j + 1) * 128].astype(BF16)
        at = place_on(self.axes[1])
        self.around(
            self.axes[1], lambda k: self.src2.at[lax.rem(at + k, 4)], lambda k: self.recv2.at[k - 1], self.recv2
        )

    def exchange3(self):
        self.arrived()
        total = self.src2[place_on(self.axes[1])].astype(F32)
        for k in range(3):
            total = total + self.recv2[k].astype(F32)
        self.buf3[0] = total.astype(BF16)
        self.around(self.axes[2], lambda k: self.buf3.at[0], lambda k: self.buf3.at[k], self.buf3.at[1:4])

    def gather2(self):
        self.arrived()
        at = place_on(self.axes[2])
        total = self.buf3[at].astype(F32)
        for s in range(1, 4):
            total = total + self.buf3[lax.rem(at + 4 - s, 4)].astype(F32)
        rows = pl.ds(pl.multiple_of(place_on(self.axes[0]) * self.piece, self.piece), self.piece)
        lanes = pl.ds(pl.multiple_of(place_on(self.axes[1]) * 128, 128), 128)
        self.result[rows, lanes] = total.astype(BF16)
        mine = self.result.at[rows, lanes]
        self.around(self.axes[1], lambda k: mine, lambda k: mine, self.recv2)

    def gather1(self):
        self.arrived()
        mine = self.result.at[pl.ds(pl.multiple_of(place_on(self.axes[0]) * self.piece, self.piece), self.piece), :]
        self.around(self.axes[0], lambda k: mine, lambda k: mine, self.recv1)

    def share(self):
        self.arrived()
        self.across(self.result, self.result)

    def settle(self):
        for copy in self.sent:
            copy.wait_send()


def sum_kernel(main_ref, out_ref, main_v, out_v, sem_in, sem_out, *scratch):
    half = lax.rem(lax.axis_index("lat"), 2)
    load = pltpu.make_async_copy(main_ref.at[half], main_v.at[half], sem_in)
    load.start()
    barrier = pltpu.get_barrier_semaphore()
    pl.semaphore_signal(barrier, inc=1, device_id=peer("core", 1), device_id_type=MESH)
    for axis in ORDER:
        for k in range(1, 4):
            pl.semaphore_signal(barrier, inc=1, device_id=peer(axis, k), device_id_type=MESH)
    jobs = []
    for i, (start, rows, turn) in enumerate(JOBS):
        jobs.append(Job(main_ref, main_v, out_v, half, start, rows, turn, scratch[7 * i : 7 * i + 6], scratch[7 * i + 6]))
    stores = []

    def store(job, i, h):
        at = pl.ds(job.start, job.rows)
        stores.append(pltpu.make_async_copy(out_v.at[h, at, :], out_ref.at[h, at, :], sem_out.at[i]))
        stores[-1].start()

    pl.semaphore_wait(barrier, 10)
    for job in jobs:
        job.swap()
    load.wait()
    for what in ("scatter1", "scatter2", "exchange3", "gather2", "gather1"):
        for job in jobs:
            getattr(job, what)()
    for i, job in enumerate(jobs):
        job.share()
        store(job, i, half)
    for i, job in enumerate(jobs):
        job.arrived()
        store(job, len(JOBS) + i, 1 - half)
    for job in jobs:
        job.settle()
    for copy in stores:
        copy.wait()


def widen_kernel(gobs_ref, gkv_ref, gqo_ref, obs_ref, kv_ref, q_ref, o_ref):
    obs_ref[...] = gobs_ref[0].astype(F32)
    q_ref[...] = gqo_ref[0].astype(F32)
    o_ref[...] = gqo_ref[1].astype(F32)
    for h in range(2):
        kv_ref[:, h * D : (h + 1) * D] = gkv_ref[h].astype(F32)


def sum_grads(main):
    far = pl.BlockSpec(memory_space=pltpu.HBM)
    dma = pltpu.SemaphoreType.DMA
    scratch = []
    for _, n, _ in JOBS:
        piece = n // 4
        scratch += [
            pltpu.VMEM((n, D), BF16),
            pltpu.VMEM((4, piece, D), BF16),
            pltpu.VMEM((3, piece, D), BF16),
            pltpu.VMEM((4, piece, 128), BF16),
            pltpu.VMEM((3, piece, 128), BF16),
            pltpu.VMEM((4, piece, 128), BF16),
            dma((7, 2)),
        ]
    return pl.pallas_call(
        sum_kernel,
        out_shape=jax.ShapeDtypeStruct((2, HALF, D), BF16),
        in_specs=[far],
        out_specs=far,
        scratch_shapes=[
            pltpu.VMEM((2, HALF, D), BF16),
            pltpu.VMEM((2, HALF, D), BF16),
            dma,
            dma((2 * len(JOBS),)),
        ] + scratch,
        compiler_params=pltpu.CompilerParams(
            collective_id=1, has_side_effects=True, vmem_limit_bytes=VMEM_LIMIT
        ),
        name="sum_grads",
    )(main)


def body(latents, d_out, observations, obs_bias, footprint, obs_cell, w_obs, w_kv, w_q, w_o):
    vmem = pl.BlockSpec(memory_space=pltpu.VMEM)
    dma = pltpu.SemaphoreType.DMA
    far = pl.BlockSpec(memory_space=pltpu.HBM)
    recv, rmeta, q, back = pl.pallas_call(
        exchange_kernel,
        out_shape=(
            jax.ShapeDtypeStruct((2, 64, 16, CH), BF16),
            jax.ShapeDtypeStruct((2, 64, 1, 128), F32),
            jax.ShapeDtypeStruct((CELLS, D), BF16),
            jax.ShapeDtypeStruct((CELLS, D), BF16),
        ),
        in_specs=[far] * 8,
        out_specs=[far] * 4,
        scratch_shapes=[
            pltpu.VMEM((4, 32), jnp.int32),
            pltpu.VMEM((32 * OBS, CH), BF16),
            pltpu.VMEM((OBS, 32), BF16),
            pltpu.VMEM((4, OBS, 32), jnp.int32),
            pltpu.VMEM((CELLS, D), BF16),
            pltpu.VMEM((CELLS, D), BF16),
            pltpu.VMEM((D, D), BF16),
            pltpu.VMEM((D, D), BF16),
            pltpu.VMEM((CELLS, D), BF16),
            pltpu.VMEM((CELLS, D), BF16),
            pltpu.VMEM((2, 64, 16, CH), BF16),
            pltpu.VMEM((2, 64, 1, 128), F32),
            pltpu.VMEM((64, 16, CH), BF16),
            pltpu.VMEM((64, 1, 128), F32),
            pltpu.VMEM((16, 128), F32),
            pltpu.VMEM((128, 1280), F32),
            dma((8,)),
            dma((4,)),
            dma((2, 2)),
            dma((3, 2)),
        ],
        compiler_params=pltpu.CompilerParams(
            collective_id=0, has_side_effects=True, vmem_limit_bytes=VMEM_LIMIT
        ),
        name="exchange",
    )(
        footprint.T, observations.reshape(-1, CH), obs_bias.T, obs_cell.transpose(1, 2, 0),
        latents, d_out, w_q, w_o,
    )
    upd, dlat, main = pl.pallas_call(
        tile_kernel,
        out_shape=(
            jax.ShapeDtypeStruct((CELLS, D), BF16),
            jax.ShapeDtypeStruct((CELLS, D), BF16),
            jax.ShapeDtypeStruct((2, HALF, D), BF16),
        ),
        in_specs=[far] * 10,
        out_specs=[far] * 3,
        scratch_shapes=[
            pltpu.VMEM((CH, MAXB * KB), BF16),
            pltpu.VMEM((MAXB * KB, D), F32),
            pltpu.VMEM((D, MAXB * KB), BF16),
            pltpu.VMEM((MAXB * KB, 2 * D), BF16),
            pltpu.VMEM((MAXB * KB, 128), F32),
            pltpu.VMEM((CELLS, D), BF16),
            pltpu.VMEM((CELLS, D), BF16),
            pltpu.VMEM((LEAD * KB, D), BF16),
            pltpu.VMEM((768, 2 * D), F32),
            pltpu.VMEM((2, HALF, D), BF16),
            pltpu.VMEM((CELLS, D), BF16),
            pltpu.VMEM((CELLS, D), BF16),
            pltpu.SMEM((3, GROUPS), jnp.int32),
            pltpu.VMEM((ROWS, CH), BF16),
            pltpu.VMEM((DEV, 128), F32),
            pltpu.VMEM((CELLS, D), BF16),
            pltpu.VMEM((CELLS, D), BF16),
            pltpu.VMEM((CELLS, D), BF16),
            pltpu.VMEM((CELLS, D), BF16),
            pltpu.VMEM((CH, D), BF16),
            pltpu.VMEM((D, 2 * D), BF16),
            pltpu.VMEM((D, D), BF16),
            pltpu.VMEM((D, D), BF16),
            dma((10,)),
            dma((3,)),
        ],
        compiler_params=pltpu.CompilerParams(vmem_limit_bytes=VMEM_LIMIT),
        name="tile",
    )(recv.reshape(ROWS, CH), rmeta.reshape(DEV, 128), q, back, latents, d_out, w_obs, w_kv, w_q, w_o)
    total = sum_grads(main)
    gobs, gkv, gq, go = pl.pallas_call(
        widen_kernel,
        grid=(4,),
        out_shape=[jax.ShapeDtypeStruct(x.shape, F32) for x in (w_obs, w_kv, w_q, w_o)],
        in_specs=[
            pl.BlockSpec((1, 64, D), lambda i: (i // 2, 16 + i % 2, 0)),
            pl.BlockSpec((2, 128, D), lambda i: (0, 4 + i, 0)),
            pl.BlockSpec((2, 128, D), lambda i: (0, i, 0)),
        ],
        out_specs=[
            pl.BlockSpec((64, D), lambda i: (i, 0)),
            pl.BlockSpec((128, 2 * D), lambda i: (i, 0)),
            pl.BlockSpec((128, D), lambda i: (i, 0)),
            pl.BlockSpec((128, D), lambda i: (i, 0)),
        ],
        compiler_params=pltpu.CompilerParams(vmem_limit_bytes=VMEM_LIMIT),
        name="widen",
    )(total, total, total)
    return upd, dlat, gobs, gkv, gq, go


def solution(mesh):
    spread = ("lat", "lon")
    placed = (
        P(spread, None), P(spread, None), P(spread, None, None), P(spread, None), P(spread, None),
        P(spread, None, None), P(), P(), P(), P(),
    )
    return jax.shard_map(
        body,
        mesh=mesh,
        in_specs=placed,
        out_specs=(P(spread, None), P(spread, None), P(), P(), P(), P()),
        check_vma=False,
    )
```

```python
import functools
import math

import jax
import jax.numpy as jnp
from jax import lax
from jax.experimental import pallas as pl
from jax.experimental.pallas import tpu as pltpu
from jax.sharding import PartitionSpec as P

HEADS = 8
GROUPS = 8
DEV = 128
OBS = 8
CAP = 2
CH = 256
D = 512
CELLS = 1024
GCELLS = CELLS // GROUPS
ROWS = DEV * CAP * OBS
KB = 128
MAXB = 24
LEAD = 18
SPAN = 768
F32 = jnp.float32
BF16 = jnp.bfloat16
NEG = -1e30
VMEM_LIMIT = 59 << 20
MESH = pl.DeviceIdType.MESH


def dot(a, b):
    return lax.dot_general(a, b, (((1,), (0,)), ((), ())), preferred_element_type=F32)


def dot_nt(a, b):
    return lax.dot_general(a, b, (((1,), (1,)), ((), ())), preferred_element_type=F32)


def dot_tn(a, b):
    return lax.dot_general(a, b, (((0,), (0,)), ((), ())), preferred_element_type=F32)


def iota(shape, dim):
    return lax.broadcasted_iota(jnp.int32, shape, dim)


def gelu_parts(x):
    a = jnp.abs(x)
    t = 1.0 / (1.0 + (0.3275911 / math.sqrt(2.0)) * a)
    e = jnp.exp(-0.5 * x * x)
    poly = t * (
        0.5 * 0.254829592
        + t * (-0.5 * 0.284496736 + t * (0.5 * 1.421413741 + t * (-0.5 * 1.453152027 + t * (0.5 * 1.061405429))))
    )
    tail = poly * e
    cdf = jnp.where(x < 0.0, tail, 1.0 - tail)
    return x * cdf, cdf + x * e * (1.0 / math.sqrt(2.0 * math.pi))


def hot(mask):
    return jnp.where(mask, 1.0, 0.0).astype(BF16)


def exchange_kernel(
    foot_ref, obs_ref, bias_ref, cell_ref, lat_ref, dout_ref, wq_ref, wo_ref,
    recv_ref, place_ref, group_ref, q_ref, back_ref,
    foot_v, obs_v, bias_v, cell_v, lat_v, dout_v, wq_v, wo_v, q_v, back_v,
    stage, mstage, rmeta, place_v, group_v, osend, omsend, foot_s, marks_s, sem_in, sem_out, sem_core, sem_chip,
):
    lat, lon = lax.axis_index("lat"), lax.axis_index("lon")
    core = lax.rem(lat, 2)
    y, z, x = lat // 2, lon // 4, lax.rem(lon, 4)
    loads = []
    for i, (src, dst) in enumerate((
        (foot_ref, foot_v), (obs_ref, obs_v), (bias_ref, bias_v), (cell_ref, cell_v),
        (lat_ref, lat_v), (wq_ref, wq_v), (dout_ref, dout_v), (wo_ref, wo_v),
    )):
        loads.append(pltpu.make_async_copy(src, dst, sem_in.at[i]))
        loads[-1].start()

    ys = [lax.rem(y + d, 4) for d in range(4)]
    lons = [lax.rem(z + d // 4, 4) * 4 + lax.rem(x + d % 4, 4) for d in range(16)]
    chips = []
    for k in range(1, 64):
        cy, cl = ys[k // 16], lons[k % 16]
        chips.append((cy * 16 + cl, {"lat": cy * 2 + core, "lon": cl}))
    sibling = {"lat": y * 2 + 1 - core, "lon": lon}
    my_chip = y * 16 + lon
    barrier = pltpu.get_barrier_semaphore()
    pl.semaphore_signal(barrier, inc=1, device_id=sibling, device_id_type=MESH)
    for chip, where in chips:
        pl.semaphore_signal(barrier, inc=1, device_id=where, device_id_type=MESH)

    foot_s[...] = jnp.full((16, 128), -1.0, F32)
    marks_s[...] = jnp.zeros((128, 1280), F32)
    for load in loads[:4]:
        load.wait()
    foot_s[0:4, 0:32] = foot_v[...].astype(F32)
    for rank in range(CAP):
        lane, at = rank * OBS, rank * 640
        marks_s[lane : lane + OBS, at : at + 32] = bias_v[...].astype(F32)
        for f in range(4):
            lane, at = (CAP + rank) * OBS, rank * 640 + (1 + f) * 128
            marks_s[lane : lane + OBS, at : at + 32] = cell_v[f].astype(F32) - float(GROUPS)
    foot = foot_s[...]
    marks = marks_s[...].astype(BF16)
    r, c = iota((128, 128), 0), iota((128, 128), 1)
    upper = hot(r < c)
    widen = hot(iota((128, 256), 1) // OBS == iota((128, 256), 0))
    keep = iota((1024, 256), 0) % OBS == iota((1024, 256), 1) % OBS

    def slots_of(to_core):
        tile = (r // 32) * 32 + to_core * 16 + (r // CAP) % 16
        hit = jnp.zeros((128, 128), F32)
        for f in range(4):
            hit = hit + jnp.where(foot[f : f + 1, :] == tile.astype(F32), 1.0, 0.0)
        sel = hit * jnp.where(dot(hit.astype(BF16), upper) == (r % CAP).astype(F32), 1.0, 0.0)
        blocks = dot(sel.astype(BF16), widen)
        spread = jnp.broadcast_to(blocks[:, None, :], (128, OBS, 256)).reshape(1024, 256)
        rows = dot(jnp.where(keep, spread, 0.0).astype(BF16), obs_v[...]).astype(BF16)
        tile = iota((64, 128), 0)
        tile = ((tile // 16) * 32 + to_core * 16 + tile % 16).astype(F32)
        hits = [jnp.where(foot[f : f + 1, :] == tile, 1.0, 0.0) for f in range(4)]
        any_hit = hits[0] + hits[1] + hits[2] + hits[3]
        order = dot(any_hit.astype(BF16), upper)
        left = []
        for rank in range(CAP):
            chosen = any_hit * jnp.where(order == float(rank), 1.0, 0.0)
            left += [chosen] + [chosen * hits[f] for f in range(4)]
        meta = dot_nt(jnp.concatenate(left, axis=1).astype(BF16), marks)
        return rows.reshape(64, 16, CH), meta.reshape(64, 1, 128)

    osend[...], omsend[...] = slots_of(1 - core)
    stage[core], mstage[core] = slots_of(core)
    pl.semaphore_wait(barrier, 64)

    def copy(src, dst, sems, where):
        return pltpu.make_async_remote_copy(
            src_ref=src, dst_ref=dst, send_sem=sems.at[0], recv_sem=sems.at[1], device_id=where, device_id_type=MESH,
        )

    swap = [copy(osend, stage.at[core], sem_core.at[0], sibling), copy(omsend, mstage.at[core], sem_core.at[1], sibling)]
    for part in swap:
        part.start()
    for chip, where in chips:
        copy(stage.at[core, chip], recv_ref.at[core, my_chip], sem_chip.at[0], where).start()
    for part in swap:
        part.wait_recv()
    for chip, where in chips:
        copy(mstage.at[:, chip], rmeta.at[:, my_chip], sem_chip.at[2], where).start()
    for chip, where in chips:
        copy(stage.at[1 - core, chip], recv_ref.at[1 - core, my_chip], sem_chip.at[1], where).start()
    rmeta[:, my_chip] = mstage[:, my_chip]
    stores = [
        pltpu.make_async_copy(stage.at[:, my_chip], recv_ref.at[:, my_chip], sem_out.at[0]),
    ]
    for store in stores:
        store.start()

    loads[4].wait()
    loads[5].wait()
    q_v[...] = (dot(lat_v[...], wq_v[...]).astype(BF16).astype(F32) * 0.125).astype(BF16)
    stores.append(pltpu.make_async_copy(q_v, q_ref, sem_out.at[2]))
    stores[-1].start()
    loads[6].wait()
    loads[7].wait()
    back_v[...] = dot_nt(dout_v[...], wo_v[...]).astype(BF16)
    stores.append(pltpu.make_async_copy(back_v, back_ref, sem_out.at[3]))
    stores[-1].start()

    whole = [
        copy(stage.at[core, 0:63], recv_ref.at[core, 0:63], sem_chip.at[0], sibling),
        copy(stage.at[1 - core, 0:63], recv_ref.at[1 - core, 0:63], sem_chip.at[1], sibling),
        copy(mstage.at[:, 0:63], rmeta.at[:, 0:63], sem_chip.at[2], sibling),
    ]
    whole[2].wait_recv()
    r, c = iota((128, 128), 0), iota((128, 128), 1)
    marks = rmeta[...].reshape(DEV, 128).astype(BF16)
    own_lane = r % 8 == c // 16
    chunk = jnp.where(iota((16, 128), 0) == iota((16, 128), 1) // 8, 1.0, 0.0).astype(BF16)

    def laned(first_lane):
        lanes = dot(marks, jnp.where(r == c % 16 + first_lane, 1.0, 0.0).astype(BF16))
        return dot(chunk, jnp.where(own_lane, lanes, 0.0).astype(BF16))

    bias_row = laned(0)
    cell = laned(16) + float(GROUPS)
    inside = jnp.concatenate([jnp.where(cell == float(g), 1.0, 0.0) for g in range(GROUPS)], axis=0)
    upto = jnp.where(r <= c, 1.0, 0.0).astype(BF16)
    prefix = dot(inside.astype(BF16), upto)
    total = jnp.broadcast_to(prefix[:, 127:128], (128, 128)).astype(BF16)
    same = r // 16 == c // 16
    before = dot(jnp.where(same & (c < r), 1.0, 0.0).astype(BF16), total)
    count = dot(jnp.where(same, 1.0, 0.0).astype(BF16), total)
    nblk = jnp.floor((count + (KB - 1.0)) * (1.0 / KB))
    first = dot(jnp.where((c % 16 == 0) & (c // 16 < r // 16), 1.0, 0.0).astype(BF16), nblk.astype(BF16))
    place = jnp.where(inside > 0.5, first * float(KB) + before + prefix - 1.0, -1.0)
    pos = place[0:16, :]
    for g in range(1, GROUPS):
        pos = jnp.maximum(pos, place[g * 16 : (g + 1) * 16, :])
    place_v[0] = pos
    place_v[1] = bias_row
    for kind, values in enumerate((first, nblk, count)):
        group_v[kind] = jnp.concatenate([values[g * 16 : g * 16 + 8, :] for g in range(GROUPS)], axis=0)
    stores.append(pltpu.make_async_copy(place_v, place_ref, sem_out.at[1]))
    stores[-1].start()
    stores.append(pltpu.make_async_copy(group_v, group_ref, sem_out.at[4]))
    stores[-1].start()
    for part in whole[:2]:
        part.wait_recv()
    for part in whole:
        part.wait_send()
    for part in swap:
        part.wait_send()
    for store in stores:
        store.wait()


def tile_kernel(
    recv_ref, place_ref, group_ref, q_ref, back_ref, lat_ref, dout_ref, wobs_ref, wkv_ref, wq_ref, wo_ref,
    upd_ref, dlat_ref, main_ref,
    rowst_s, slope_s, enct_s, kv_s, bias_s, attn_s, dq_s, dpre_s, sums_s, main_v, upd_v, dlat_v, meta_sm,
    recv_v, place_v, group_v, q_s, back_s, lat_v, dout_v, wobs_v, wkv_v, wq_v, wo_v, sem_in, sem_out,
):
    loads = []
    for i, (src, dst) in enumerate((
        (group_ref, group_v), (place_ref, place_v), (recv_ref, recv_v), (wobs_ref, wobs_v), (wkv_ref, wkv_v), (q_ref, q_s), (back_ref, back_s),
        (lat_ref, lat_v), (dout_ref, dout_v), (wq_ref, wq_v), (wo_ref, wo_v),
    )):
        loads.append(pltpu.make_async_copy(src, dst, sem_in.at[i]))
        loads[-1].start()

    loads[0].wait()
    loads[1].wait()
    pos, bias_row = place_v[0], place_v[1]
    for g in range(GROUPS):
        for kind in range(3):
            meta_sm[kind, g] = jnp.max(group_v[kind, g * 8 : g * 8 + 8, :]).astype(jnp.int32)
    blocks = meta_sm[0, GROUPS - 1] + meta_sm[1, GROUPS - 1]

    lane_pos = [jnp.broadcast_to(pos[i : i + 1, :], (16, 128)) for i in range(16)]
    lane_bias = [jnp.broadcast_to(bias_row[i : i + 1, :], (16, 128)).astype(BF16) for i in range(16)]
    row_id = iota((256, 128), 0).astype(F32).astype(BF16)

    def gather(base, rows):
        cols = []
        bias = jnp.zeros((rows, 128), BF16)
        for i in range(16):
            rel = jnp.clip(lane_pos[i] - base, -1.0, float(rows)).astype(BF16)
            found = row_id[0:rows] == jnp.concatenate([rel] * (rows // 16), axis=0)
            cols.append(jnp.where(found, jnp.ones((), BF16), jnp.zeros((), BF16)))
            bias = jnp.where(found, jnp.concatenate([lane_bias[i]] * (rows // 16), axis=0), bias)
        bias = jnp.sum(bias.astype(F32), axis=1, keepdims=True)
        return jnp.concatenate(cols, axis=1), jnp.broadcast_to(bias, (rows, 128))

    def picked(at, picks):
        bias_s[at, :] = jnp.concatenate([pick[1] for pick in picks], axis=0)
        rows = dot(jnp.concatenate([pick[0] for pick in picks], axis=0), recv_v[...]).astype(BF16)
        rowst_s[:, at] = rows.T
        return dot(rows, wobs_v[...])

    def encoded(at, pre):
        value, slope = gelu_parts(pre)
        enc = value.astype(BF16)
        slope_s[at, :] = slope
        enct_s[:, at] = enc.T
        kv_s[at, :] = dot(enc, wkv_v[...]).astype(BF16)

    for load in loads[2:5]:
        load.wait()
    last = None
    for i in range(LEAD * KB // SPAN):
        at = slice(i * SPAN, (i + 1) * SPAN)
        pre = picked(at, [gather(float(i * SPAN + j), 256) for j in range(0, SPAN, 256)])
        if last is not None:
            encoded(*last)
        last = (at, pre)
    encoded(*last)

    def encode(b, carry):
        at = pl.ds(pl.multiple_of(b * KB, KB), KB)
        encoded(at, picked(at, [gather((b * KB).astype(F32), KB)]))
        return carry

    lax.fori_loop(LEAD, blocks, encode, 0)
    for load in loads[5:7]:
        load.wait()

    lane_head = iota((GCELLS, 256), 1) // 64

    def spread_heads(x):
        return jnp.concatenate([jnp.where(lane_head == h, x, jnp.zeros((), BF16)) for h in range(4)], axis=0)

    def scores(r0, rows, valid, half, qq):
        keys = kv_s[pl.ds(r0, rows), half * 256 : half * 256 + 256]
        bias = jnp.where(iota((rows, 128), 0) < valid, bias_s[pl.ds(r0, rows), :], NEG)
        return dot_nt(keys, qq) + jnp.concatenate([bias] * 4, axis=1)

    def dprobs(r0, rows, half, bb):
        return dot_nt(kv_s[pl.ds(r0, rows), D + half * 256 : D + half * 256 + 256], bb)

    def diagonal(x):
        out = x[0:GCELLS]
        for h in range(1, 4):
            out = jnp.where(lane_head == h, x[h * GCELLS : (h + 1) * GCELLS], out)
        return out

    def products(r0, rows, half, wb, ds, qq, bb):
        keys = kv_s[pl.ds(r0, rows), half * 256 : half * 256 + 256]
        values = kv_s[pl.ds(r0, rows), D + half * 256 : D + half * 256 + 256]
        attn = diagonal(dot(wb.T, values))
        dq = diagonal(dot(ds.T, keys))
        return attn, dq, dot(ds, qq).astype(BF16), dot(wb, bb).astype(BF16)

    def put_keys(r0, rows, half, dk, dv):
        kv_s[pl.ds(r0, rows), half * 256 : half * 256 + 256] = dk
        kv_s[pl.ds(r0, rows), D + half * 256 : D + half * 256 + 256] = dv

    def heads(c0, half):
        lanes = slice(half * 256, half * 256 + 256)
        return spread_heads(q_s[pl.ds(c0, GCELLS), lanes]), spread_heads(back_s[pl.ds(c0, GCELLS), lanes])

    def put(c0, half, attn, dq):
        lanes = slice(half * 256, half * 256 + 256)
        attn_s[pl.ds(c0, GCELLS), lanes] = attn.astype(BF16)
        dq_s[pl.ds(c0, GCELLS), lanes] = (dq * 0.125).astype(BF16)

    def at_once(groups, rows):
        jobs = []
        for g in groups:
            r0, c0 = pl.multiple_of(meta_sm[0, g] * KB, KB), pl.multiple_of(g * GCELLS, GCELLS)
            for half in range(2):
                jobs.append((r0, c0, half, meta_sm[2, g]) + heads(c0, half))
        raw = [scores(r0, rows, valid, half, qq) for r0, _, half, valid, qq, _ in jobs]
        dps = [dprobs(r0, rows, half, bb) for r0, _, half, _, _, bb in jobs]
        done = []
        for (r0, _, half, _, qq, bb), s, dp in zip(jobs, raw, dps):
            top = jnp.maximum(jnp.max(s, axis=0, keepdims=True), 0.0)
            p = jnp.exp(s - top)
            inv = 1.0 / (jnp.exp(-top) + jnp.sum(p, axis=0, keepdims=True))
            weights = p * inv
            delta = jnp.sum(weights * dp, axis=0, keepdims=True)
            wb, ds = weights.astype(BF16), (weights * (dp - delta)).astype(BF16)
            done.append(products(r0, rows, half, wb, ds, qq, bb))
        for (r0, c0, half, _, _, _), (attn, dq, dk, dv) in zip(jobs, done):
            put_keys(r0, rows, half, dk, dv)
            put(c0, half, attn, dq)

    def by_chunks(g):
        start, nb, count = meta_sm[0, g], meta_sm[1, g], meta_sm[2, g]
        c0 = pl.multiple_of(g * GCELLS, GCELLS)
        for half in range(2):
            qq, bb = heads(c0, half)

            def row(b):
                return pl.multiple_of((start + b) * KB, KB)

            def score(b):
                return scores(row(b), KB, count - b * KB, half, qq)

            def first_pass(b, top):
                return jnp.maximum(top, jnp.max(score(b), axis=0, keepdims=True))

            top = lax.fori_loop(0, nb, first_pass, jnp.zeros((1, 512), F32))

            def second_pass(b, sums):
                p = jnp.exp(score(b) - top)
                dp = dprobs(row(b), KB, half, bb)
                return (
                    sums[0] + jnp.sum(p, axis=0, keepdims=True),
                    sums[1] + jnp.sum(p * dp, axis=0, keepdims=True),
                )

            sums = lax.fori_loop(0, nb, second_pass, (jnp.exp(-top), jnp.zeros((1, 512), F32)))
            inv = 1.0 / sums[0]
            delta = sums[1] * inv

            def third_pass(b, acc):
                weights = jnp.exp(score(b) - top) * inv
                dp = dprobs(row(b), KB, half, bb)
                wb, ds = weights.astype(BF16), (weights * (dp - delta)).astype(BF16)
                attn, dq, dk, dv = products(row(b), KB, half, wb, ds, qq, bb)
                put_keys(row(b), KB, half, dk, dv)
                return acc[0] + attn, acc[1] + dq

            zero = jnp.zeros((GCELLS, 256), F32)
            put(c0, half, *lax.fori_loop(0, nb, third_pass, (zero, zero)))

    def single(g):
        nb = meta_sm[1, g]
        for size in (1, 2, 3):

            @pl.when(nb == size)
            def _():
                at_once((g,), size * KB)

        @pl.when((nb < 1) | (nb > 3))
        def _():
            by_chunks(g)

    def pair(i, carry):
        one, two = 2 * i, 2 * i + 1
        alike = (meta_sm[1, one] == 2) & (meta_sm[1, two] == 2)

        @pl.when(alike)
        def _():
            at_once((one, two), 2 * KB)

        @pl.when(jnp.logical_not(alike))
        def _():
            lax.fori_loop(one, two + 1, lambda g, c: (single(g), c)[1], 0)

        return carry

    lax.fori_loop(0, GROUPS // 2, pair, 0)

    for load in loads[7:]:
        load.wait()
    attn, dq = attn_s[...], dq_s[...]
    outs = []

    def put_out(src, dst):
        outs.append(pltpu.make_async_copy(src, dst, sem_out.at[len(outs)]))
        outs[-1].start()

    upd_v[...] = (lat_v[...].astype(F32) + dot(attn, wo_v[...])).astype(BF16)
    put_out(upd_v, upd_ref)
    dlat_v[...] = (dout_v[...].astype(F32) + dot_nt(dq, wq_v[...])).astype(BF16)
    put_out(dlat_v, dlat_ref)
    main_v[0, 0:512, :] = dot_tn(lat_v[...], dq).astype(BF16)
    main_v[1, 0:512, :] = dot_tn(attn, dout_v[...]).astype(BF16)
    put_out(main_v.at[:, 0:512, :], main_ref.at[:, 0:512, :])

    def through_encoder(at):
        return (dot_nt(kv_s[at, :], wkv_v[...]) * slope_s[at, :]).astype(BF16)

    lead = LEAD * KB
    for i in range(lead // SPAN):
        dpre_s[i * SPAN : (i + 1) * SPAN, :] = through_encoder(slice(i * SPAN, (i + 1) * SPAN))

    def lead_kv(i):
        return dot(enct_s[:, 0:lead], kv_s[0:lead, i * 256 : (i + 1) * 256])

    lead_obs = dot(rowst_s[:, 0:lead], dpre_s[...])

    @pl.when(blocks <= LEAD)
    def _():
        for i in range(4):
            main_v[i // 2, 512:1024, i % 2 * 256 : i % 2 * 256 + 256] = lead_kv(i).astype(BF16)
        for h in range(2):
            main_v[h, 1024:1152, :] = lead_obs[h * 128 : (h + 1) * 128].astype(BF16)

    @pl.when(blocks > LEAD)
    def _():
        for i in range(4):
            sums_s[0:512, i * 256 : (i + 1) * 256] = lead_kv(i)
        sums_s[512:768, 0:512] = lead_obs

        def encoder_grads(b, carry):
            at = pl.ds(pl.multiple_of(b * KB, KB), KB)
            sums_s[0:512, :] += dot(enct_s[:, at], kv_s[at, :])
            sums_s[512:768, 0:512] += dot(rowst_s[:, at], through_encoder(at))
            return carry

        lax.fori_loop(LEAD, blocks, encoder_grads, 0)
        for h in range(2):
            main_v[h, 512:1024, :] = sums_s[0:512, h * 512 : (h + 1) * 512].astype(BF16)
            main_v[h, 1024:1152, :] = sums_s[512 + h * 128 : 640 + h * 128, 0:512].astype(BF16)

    put_out(main_v.at[:, 512:HALF, :], main_ref.at[:, 512:HALF, :])
    for out in outs:
        out.wait()


ORDER = ("x", "y", "z")
JOBS = tuple((i * 128, 128, i % 3) for i in range(9))
HALF = 1152


def peer(step_axis, k):
    lat, lon = lax.axis_index("lat"), lax.axis_index("lon")
    y, core, z, x = lat // 2, lat % 2, lon // 4, lon % 4
    if step_axis == "x":
        x = (x + k) % 4
    elif step_axis == "y":
        y = (y + k) % 4
    elif step_axis == "z":
        z = (z + k) % 4
    else:
        core = 1 - core
    return {"lat": y * 2 + core, "lon": z * 4 + x}


def place_on(step_axis):
    lat, lon = lax.axis_index("lat"), lax.axis_index("lon")
    return {"x": lon % 4, "y": lat // 2, "z": lon // 4}[step_axis]


class Job:
    def __init__(self, far, near, out, half, start, rows, turn, bufs, sems):
        self.far, self.near, self.start, self.rows, self.piece = far, near, start, rows, rows // 4
        self.axes = [ORDER[(turn + i) % 3] for i in range(3)]
        self.core_recv, self.src1, self.recv1, self.src2, self.recv2, self.buf3 = bufs
        self.sems, self.half, self.phase, self.sent = sems, half, -1, []
        self.result = out.at[half, pl.ds(start, rows), :]

    def describe(self, src, dst, axis, k):
        return pltpu.make_async_remote_copy(
            src_ref=src, dst_ref=dst, send_sem=self.sems.at[self.phase, 0], recv_sem=self.sems.at[self.phase, 1],
            device_id=peer(axis, k), device_id_type=MESH,
        )

    def across(self, src, dst):
        self.phase += 1
        copy = self.describe(src, dst, "core", 1)
        copy.start()
        self.sent.append(copy)

    def around(self, axis, src_of, dst_of, whole):
        self.phase += 1
        for k in range(1, 4):
            self.describe(src_of(k), dst_of(k), axis, k).start()
        self.sent.append(self.describe(whole, whole, axis, 1))

    def arrived(self):
        self.sent[-1].wait_recv()

    def swap(self):
        self.across(self.far.at[1 - self.half, pl.ds(self.start, self.rows), :], self.core_recv)

    def scatter1(self):
        self.arrived()
        own = self.near[self.half, self.start : self.start + self.rows, :].astype(F32)
        total = (own + self.core_recv[...].astype(F32)).astype(BF16)
        for j in range(4):
            self.src1[j] = total[j * self.piece : (j + 1) * self.piece, :]
        at = place_on(self.axes[0])
        self.around(
            self.axes[0], lambda k: self.src1.at[lax.rem(at + k, 4)], lambda k: self.recv1.at[k - 1], self.recv1
        )

    def scatter2(self):
        self.arrived()
        total = self.src1[place_on(self.axes[0])].astype(F32)
        for k in range(3):
            total = total + self.recv1[k].astype(F32)
        for j in range(4):
            self.src2[j] = total[:, j * 128 : (j + 1) * 128].astype(BF16)
        at = place_on(self.axes[1])
        self.around(
            self.axes[1], lambda k: self.src2.at[lax.rem(at + k, 4)], lambda k: self.recv2.at[k - 1], self.recv2
        )

    def exchange3(self):
        self.arrived()
        total = self.src2[place_on(self.axes[1])].astype(F32)
        for k in range(3):
            total = total + self.recv2[k].astype(F32)
        self.buf3[0] = total.astype(BF16)
        self.around(self.axes[2], lambda k: self.buf3.at[0], lambda k: self.buf3.at[k], self.buf3.at[1:4])

    def gather2(self):
        self.arrived()
        at = place_on(self.axes[2])
        total = self.buf3[at].astype(F32)
        for s in range(1, 4):
            total = total + self.buf3[lax.rem(at + 4 - s, 4)].astype(F32)
        rows = pl.ds(pl.multiple_of(place_on(self.axes[0]) * self.piece, self.piece), self.piece)
        lanes = pl.ds(pl.multiple_of(place_on(self.axes[1]) * 128, 128), 128)
        self.result[rows, lanes] = total.astype(BF16)
        mine = self.result.at[rows, lanes]
        self.around(self.axes[1], lambda k: mine, lambda k: mine, self.recv2)

    def gather1(self):
        self.arrived()
        mine = self.result.at[pl.ds(pl.multiple_of(place_on(self.axes[0]) * self.piece, self.piece), self.piece), :]
        self.around(self.axes[0], lambda k: mine, lambda k: mine, self.recv1)

    def share(self):
        self.arrived()
        self.across(self.result, self.result)

    def settle(self):
        for copy in self.sent:
            copy.wait_send()


def sum_kernel(main_ref, out_ref, main_v, out_v, sem_in, sem_out, *scratch):
    half = lax.rem(lax.axis_index("lat"), 2)
    load = pltpu.make_async_copy(main_ref.at[half], main_v.at[half], sem_in)
    load.start()
    barrier = pltpu.get_barrier_semaphore()
    pl.semaphore_signal(barrier, inc=1, device_id=peer("core", 1), device_id_type=MESH)
    for axis in ORDER:
        for k in range(1, 4):
            pl.semaphore_signal(barrier, inc=1, device_id=peer(axis, k), device_id_type=MESH)
    jobs = []
    for i, (start, rows, turn) in enumerate(JOBS):
        jobs.append(Job(main_ref, main_v, out_v, half, start, rows, turn, scratch[7 * i : 7 * i + 6], scratch[7 * i + 6]))
    stores = []

    def store(job, i, h):
        at = pl.ds(job.start, job.rows)
        stores.append(pltpu.make_async_copy(out_v.at[h, at, :], out_ref.at[h, at, :], sem_out.at[i]))
        stores[-1].start()

    pl.semaphore_wait(barrier, 10)
    for job in jobs:
        job.swap()
    load.wait()
    for what in ("scatter1", "scatter2", "exchange3", "gather2", "gather1"):
        for job in jobs:
            getattr(job, what)()
    for i, job in enumerate(jobs):
        job.share()
        store(job, i, half)
    for i, job in enumerate(jobs):
        job.arrived()
        store(job, len(JOBS) + i, 1 - half)
    for job in jobs:
        job.settle()
    for copy in stores:
        copy.wait()


def widen_kernel(gobs_ref, gkv_ref, gqo_ref, obs_ref, kv_ref, q_ref, o_ref):
    obs_ref[...] = gobs_ref[0].astype(F32)
    q_ref[...] = gqo_ref[0].astype(F32)
    o_ref[...] = gqo_ref[1].astype(F32)
    for h in range(2):
        kv_ref[:, h * D : (h + 1) * D] = gkv_ref[h].astype(F32)


def sum_grads(main):
    far = pl.BlockSpec(memory_space=pltpu.HBM)
    dma = pltpu.SemaphoreType.DMA
    scratch = []
    for _, n, _ in JOBS:
        piece = n // 4
        scratch += [
            pltpu.VMEM((n, D), BF16),
            pltpu.VMEM((4, piece, D), BF16),
            pltpu.VMEM((3, piece, D), BF16),
            pltpu.VMEM((4, piece, 128), BF16),
            pltpu.VMEM((3, piece, 128), BF16),
            pltpu.VMEM((4, piece, 128), BF16),
            dma((7, 2)),
        ]
    return pl.pallas_call(
        sum_kernel,
        out_shape=jax.ShapeDtypeStruct((2, HALF, D), BF16),
        in_specs=[far],
        out_specs=far,
        scratch_shapes=[
            pltpu.VMEM((2, HALF, D), BF16),
            pltpu.VMEM((2, HALF, D), BF16),
            dma,
            dma((2 * len(JOBS),)),
        ] + scratch,
        compiler_params=pltpu.CompilerParams(
            collective_id=1, has_side_effects=True, vmem_limit_bytes=VMEM_LIMIT
        ),
        name="sum_grads",
    )(main)


def body(latents, d_out, observations, obs_bias, footprint, obs_cell, w_obs, w_kv, w_q, w_o):
    vmem = pl.BlockSpec(memory_space=pltpu.VMEM)
    dma = pltpu.SemaphoreType.DMA
    far = pl.BlockSpec(memory_space=pltpu.HBM)
    recv, place, group, q, back = pl.pallas_call(
        exchange_kernel,
        out_shape=(
            jax.ShapeDtypeStruct((2, 64, 16, CH), BF16),
            jax.ShapeDtypeStruct((2, 16, 128), F32),
            jax.ShapeDtypeStruct((3, 64, 128), F32),
            jax.ShapeDtypeStruct((CELLS, D), BF16),
            jax.ShapeDtypeStruct((CELLS, D), BF16),
        ),
        in_specs=[far] * 8,
        out_specs=[far] * 5,
        scratch_shapes=[
            pltpu.VMEM((4, 32), jnp.int32),
            pltpu.VMEM((32 * OBS, CH), BF16),
            pltpu.VMEM((OBS, 32), BF16),
            pltpu.VMEM((4, OBS, 32), jnp.int32),
            pltpu.VMEM((CELLS, D), BF16),
            pltpu.VMEM((CELLS, D), BF16),
            pltpu.VMEM((D, D), BF16),
            pltpu.VMEM((D, D), BF16),
            pltpu.VMEM((CELLS, D), BF16),
            pltpu.VMEM((CELLS, D), BF16),
            pltpu.VMEM((2, 64, 16, CH), BF16),
            pltpu.VMEM((2, 64, 1, 128), F32),
            pltpu.VMEM((2, 64, 1, 128), F32),
            pltpu.VMEM((2, 16, 128), F32),
            pltpu.VMEM((3, 64, 128), F32),
            pltpu.VMEM((64, 16, CH), BF16),
            pltpu.VMEM((64, 1, 128), F32),
            pltpu.VMEM((16, 128), F32),
            pltpu.VMEM((128, 1280), F32),
            dma((8,)),
            dma((5,)),
            dma((2, 2)),
            dma((3, 2)),
        ],
        compiler_params=pltpu.CompilerParams(
            collective_id=0, has_side_effects=True, vmem_limit_bytes=VMEM_LIMIT
        ),
        name="exchange",
    )(
        footprint.T, observations.reshape(-1, CH), obs_bias.T, obs_cell.transpose(1, 2, 0),
        latents, d_out, w_q, w_o,
    )
    upd, dlat, main = pl.pallas_call(
        tile_kernel,
        out_shape=(
            jax.ShapeDtypeStruct((CELLS, D), BF16),
            jax.ShapeDtypeStruct((CELLS, D), BF16),
            jax.ShapeDtypeStruct((2, HALF, D), BF16),
        ),
        in_specs=[far] * 11,
        out_specs=[far] * 3,
        scratch_shapes=[
            pltpu.VMEM((CH, MAXB * KB), BF16),
            pltpu.VMEM((MAXB * KB, D), F32),
            pltpu.VMEM((D, MAXB * KB), BF16),
            pltpu.VMEM((MAXB * KB, 2 * D), BF16),
            pltpu.VMEM((MAXB * KB, 128), F32),
            pltpu.VMEM((CELLS, D), BF16),
            pltpu.VMEM((CELLS, D), BF16),
            pltpu.VMEM((LEAD * KB, D), BF16),
            pltpu.VMEM((768, 2 * D), F32),
            pltpu.VMEM((2, HALF, D), BF16),
            pltpu.VMEM((CELLS, D), BF16),
            pltpu.VMEM((CELLS, D), BF16),
            pltpu.SMEM((3, GROUPS), jnp.int32),
            pltpu.VMEM((ROWS, CH), BF16),
            pltpu.VMEM((2, 16, 128), F32),
            pltpu.VMEM((3, 64, 128), F32),
            pltpu.VMEM((CELLS, D), BF16),
            pltpu.VMEM((CELLS, D), BF16),
            pltpu.VMEM((CELLS, D), BF16),
            pltpu.VMEM((CELLS, D), BF16),
            pltpu.VMEM((CH, D), BF16),
            pltpu.VMEM((D, 2 * D), BF16),
            pltpu.VMEM((D, D), BF16),
            pltpu.VMEM((D, D), BF16),
            dma((11,)),
            dma((4,)),
        ],
        compiler_params=pltpu.CompilerParams(vmem_limit_bytes=VMEM_LIMIT),
        name="tile",
    )(recv.reshape(ROWS, CH), place, group, q, back, latents, d_out, w_obs, w_kv, w_q, w_o)
    total = sum_grads(main)
    gobs, gkv, gq, go = pl.pallas_call(
        widen_kernel,
        grid=(4,),
        out_shape=[jax.ShapeDtypeStruct(x.shape, F32) for x in (w_obs, w_kv, w_q, w_o)],
        in_specs=[
            pl.BlockSpec((1, 64, D), lambda i: (i // 2, 16 + i % 2, 0)),
            pl.BlockSpec((2, 128, D), lambda i: (0, 4 + i, 0)),
            pl.BlockSpec((2, 128, D), lambda i: (0, i, 0)),
        ],
        out_specs=[
            pl.BlockSpec((64, D), lambda i: (i, 0)),
            pl.BlockSpec((128, 2 * D), lambda i: (i, 0)),
            pl.BlockSpec((128, D), lambda i: (i, 0)),
            pl.BlockSpec((128, D), lambda i: (i, 0)),
        ],
        compiler_params=pltpu.CompilerParams(vmem_limit_bytes=VMEM_LIMIT),
        name="widen",
    )(total, total, total)
    return upd, dlat, gobs, gkv, gq, go


def solution(mesh):
    spread = ("lat", "lon")
    placed = (
        P(spread, None), P(spread, None), P(spread, None, None), P(spread, None), P(spread, None),
        P(spread, None, None), P(), P(), P(), P(),
    )
    return jax.shard_map(
        body,
        mesh=mesh,
        in_specs=placed,
        out_specs=(P(spread, None), P(spread, None), P(), P(), P(), P()),
        check_vma=False,
    )
```
